32 devices in a mesh: dp: 2 (over core), lon: 4 (over y, x), lat: 4 (over z).
Axes of the slice: x: 2, y: 2, z: 4, core: 2. Of those that a mesh axis runs over, the one named last changes fastest.
Arguments:
- frames: bfloat16 [4, 92, 180, 768], P('dp', 'lat', 'lon'), may hold values from -6 to 6
- regions: int32 [4, 4], P('dp'), may hold values from 0 to 180, as said below
- cotangent: bfloat16 [4, 92, 180, 768], P('dp', 'lat', 'lon'), may hold values from -6 to 6
- first_gain: bfloat16 [768], replicated, may hold values from 0.5 to 1.5
- first_shift: bfloat16 [768], replicated, may hold values from -1.75 to 1.75
- inner_weight: bfloat16 [8, 2, 96, 96], replicated, may hold values from -0.4375 to 0.4375
- inner_bias: bfloat16 [8, 2, 96], replicated, may hold values from -1.75 to 1.75
- outer_weight: bfloat16 [8, 2, 96, 96], replicated, may hold values from -0.4375 to 0.4375
- outer_bias: bfloat16 [8, 2, 96], replicated, may hold values from -1.75 to 1.75
- second_gain: bfloat16 [768], replicated, may hold values from 0.5 to 1.5
- second_shift: bfloat16 [768], replicated, may hold values from -1.75 to 1.75
- hidden_weight: bfloat16 [3072, 768], P(('dp', 'lon', 'lat')), may hold values from -0.21875 to 0.21875
- hidden_bias: bfloat16 [3072], P(('dp', 'lon', 'lat')), may hold values from -1.75 to 1.75
- output_weight: bfloat16 [3072, 768], P(('dp', 'lon', 'lat')), may hold values from -0.109375 to 0.109375
- output_bias: bfloat16 [768], replicated, may hold values from -1.75 to 1.75
Outputs:
- mixed_frames: bfloat16 [4, 92, 180, 768], P('dp', 'lat', 'lon')
- frame_grad: bfloat16 [4, 92, 180, 768], P('dp', 'lat', 'lon')
- first_gain_grad: float32 [768], replicated
- first_shift_grad: float32 [768], replicated
- inner_weight_grad: float32 [8, 2, 96, 96], replicated
- inner_bias_grad: float32 [8, 2, 96], replicated
- outer_weight_grad: float32 [8, 2, 96, 96], replicated
- outer_bias_grad: float32 [8, 2, 96], replicated
- second_gain_grad: float32 [768], replicated
- second_shift_grad: float32 [768], replicated
- hidden_weight_grad: float32 [3072, 768], P(('dp', 'lon', 'lat'))
- hidden_bias_grad: float32 [3072], P(('dp', 'lon', 'lat'))
- output_weight_grad: float32 [3072, 768], P(('dp', 'lon', 'lat'))
- output_bias_grad: float32 [768], replicated
The draws below stay inside these ranges and needn't reach their ends.
Inputs may be any that keep to these rules, and one draw needn't show every extreme that they name: `regions`: row n is (latitude start, latitude count, longitude start, longitude count); latitude start + latitude count <= 90, latitude count at least 45, longitude count from 90 to 180, the longitude band wraps around; one frame covers the whole grid of 90 x 180.
All inputs are finite; a program needn't handle non-finite values.
Results may differ from the reference program's by a relative error of at most 0.019.
The reference program's roundings to bfloat16 on the way count: a program that leaves them out, or rounds other values in their place, can miss the bound.
Values may be sent and summed in bfloat16 or wider, within the bound.
No kernel may reach another device: no remote copies, remote signals or barrier semaphores. Data moves between devices by JAX's collectives and lax.ppermute only.
A program may use at most 320 MiB of HBM per device.

```python
import math
import jax
import jax.numpy as jnp
from jax import lax

D = 768
FF = 3072
BLOCKS = 8
BSIZE = 96
H = 90
W = 180
HP = 92
FRAMES = 4


def draw_regions(key, part):
    key = jax.random.fold_in(key, 11)
    subkeys = jax.random.split(key, 5)
    lat_size = jax.random.randint(subkeys[0], (FRAMES,), H // 2, H + 1)
    lat_start = jax.random.randint(subkeys[1], (FRAMES,), 0, H + 1 - lat_size)
    lon_size = jax.random.randint(subkeys[2], (FRAMES,), W // 2, W + 1)
    lon_start = jax.random.randint(subkeys[3], (FRAMES,), 0, W)
    full_frame = jax.random.randint(subkeys[4], (), 0, FRAMES)
    chosen = jnp.arange(FRAMES) == full_frame
    lat_size = jnp.where(chosen, H, lat_size)
    lat_start = jnp.where(chosen, 0, lat_start)
    lon_size = jnp.where(chosen, W, lon_size)
    return jnp.stack([lat_start, lat_size, lon_start, lon_size], axis=1).astype(jnp.int32)


def block_scale(rng, shape, shards, low, largest):
    def one(dim, shards_of):
        heights = jax.random.uniform(jax.random.fold_in(jax.random.fold_in(rng, 6), dim), (shards_of,), jnp.float32, low / len(shards), largest / len(shards))
        return jnp.repeat(jnp.exp(heights), shape[dim] // shards_of).reshape((-1,) + (1,) * (len(shape) - dim - 1))

    loudness = one(*shards[0])
    for cut in shards[1:]:
        loudness = loudness * one(*cut)
    return loudness


def gaussian(stream_key, extent, width, bound, shards=(), kind=jnp.bfloat16):
    values = jax.random.normal(stream_key, extent, jnp.float32) * width
    if len(shards) > 0:
        values = block_scale(stream_key, extent, shards, -0.22, 0.18) * values
    return jnp.clip(values, min=-bound, max=bound).astype(kind)


def setup_inputs(seed: int = 0) -> dict:
    arg_keys = jax.random.split(jax.random.key(seed), 16)
    return {
        "frames": gaussian(arg_keys[0], (FRAMES, HP, W, D), 1.0, 6.0, ((0, 2), (1, 4), (2, 4))),
        "regions": draw_regions(jax.random.fold_in(arg_keys[15], 71), 0),
        "cotangent": gaussian(arg_keys[2], (FRAMES, HP, W, D), 1.0, 6.0, ((0, 2), (1, 4), (2, 4))),
        "first_gain": jnp.clip(1.0 + 0.1 * jax.random.normal(arg_keys[3], (D,), jnp.float32), 0.5, 1.5).astype(jnp.bfloat16),
        "first_shift": gaussian(arg_keys[4], (D,), 0.3, 1.75),
        "inner_weight": gaussian(arg_keys[5], (BLOCKS, 2, BSIZE, BSIZE), (2 * BSIZE) ** -0.5, 0.4375),
        "inner_bias": gaussian(arg_keys[6], (BLOCKS, 2, BSIZE), 0.3, 1.75),
        "outer_weight": gaussian(arg_keys[7], (BLOCKS, 2, BSIZE, BSIZE), (2 * BSIZE) ** -0.5, 0.4375),
        "outer_bias": gaussian(arg_keys[8], (BLOCKS, 2, BSIZE), 0.3, 1.75),
        "second_gain": jnp.clip(1.0 + 0.1 * jax.random.normal(arg_keys[9], (D,), jnp.float32), 0.5, 1.5).astype(jnp.bfloat16),
        "second_shift": gaussian(arg_keys[10], (D,), 0.3, 1.75),
        "hidden_weight": gaussian(arg_keys[11], (FF, D), D ** -0.5, 0.21875, ((0, 32),)),
        "hidden_bias": gaussian(arg_keys[12], (FF,), 0.3, 1.75, ((0, 32),)),
        "output_weight": gaussian(arg_keys[13], (FF, D), FF ** -0.5, 0.109375, ((0, 32),)),
        "output_bias": gaussian(arg_keys[14], (D,), 0.3, 1.75),
    }


@jax.custom_vjp
def low(v):
    return lax.optimization_barrier(v.astype(jnp.bfloat16)).astype(jnp.float32)

@jax.custom_vjp
def low_back(v):
    return v

def low_keep(v):
    return (low(v), None)

def low_pass(kept, grad):
    return (grad,)

def back_keep(v):
    return (v, None)

def back_low(kept, grad):
    return (low(grad),)
low.defvjp(low_keep, low_pass)
low_back.defvjp(back_keep, back_low)
epsilon = 1e-05
shrink_level = 0.01
highest = lax.Precision.HIGHEST

def product(form, left, right):
    return jnp.einsum(form, left, right, precision=highest)

def round_both(value):
    return low_back(low(value))

def tables(count, total):
    index = jnp.arange(total, dtype=jnp.int32)
    turns = index[:, None] * index[None, :] % count
    angle = turns.astype(jnp.float32) * (2.0 * math.pi / count)
    valid = (index < count).astype(jnp.float32)
    keep = valid[:, None] * valid[None, :]
    return (jnp.cos(angle).astype(jnp.bfloat16).astype(jnp.float32) * keep, jnp.sin(angle).astype(jnp.bfloat16).astype(jnp.float32) * keep)

def layer_norm(values, gain, shift):
    centre = lax.optimization_barrier(jnp.mean(values, axis=-1, keepdims=True))
    centred = values - centre
    spread = lax.optimization_barrier(jnp.mean(centred * centred, axis=-1, keepdims=True))
    return centred * lax.rsqrt(spread + epsilon) * gain + shift

def smooth_gelu(values):
    return jax.nn.gelu(values, approximate=False)

def shrink(values):
    return values - shrink_level * values * lax.rsqrt(values * values + shrink_level * shrink_level)

def region_mask(region, height, breadth):
    lat_index = jnp.arange(height, dtype=jnp.int32)
    lon_index = jnp.arange(breadth, dtype=jnp.int32)
    lat_in = (lat_index >= region[0]) & (lat_index < region[0] + region[1])
    lon_in = (lon_index - region[2]) % breadth < region[3]
    return (lat_in[:, None] & lon_in[None, :]).astype(jnp.float32)

def complex_mix(real, imag, weight, bias):
    out_real = product('hkbi,bio->hkbo', real, weight[:, 0]) - product('hkbi,bio->hkbo', imag, weight[:, 1]) + bias[:, 0]
    out_imag = product('hkbi,bio->hkbo', imag, weight[:, 0]) + product('hkbi,bio->hkbo', real, weight[:, 1]) + bias[:, 1]
    return (out_real, out_imag)

def frame_forward(one_frame, region, weights, cos_lon, sin_lon, cos_lat, sin_lat):
    first_gain, first_shift, inner_weight, inner_bias, outer_weight, outer_bias, second_gain, second_shift, hidden_weight, hidden_bias, output_weight, output_bias = weights
    height, breadth, channels = one_frame.shape
    blocks = inner_weight.shape[0]
    block_size = channels // blocks
    inside_mask = region_mask(region, height, breadth)[:, :, None]
    inside = one_frame * inside_mask
    normed = layer_norm(inside, first_gain, first_shift)
    low_normed = low(normed)
    lon_real = round_both(product('hwc,wk->hkc', low_normed, cos_lon))
    lon_imag = round_both(-product('hwc,wk->hkc', low_normed, sin_lon))
    norm_scale = 1.0 / math.sqrt(H * breadth)
    freq_real = round_both(norm_scale * (product('qh,hkc->qkc', cos_lat, lon_real) + product('qh,hkc->qkc', sin_lat, lon_imag)))
    freq_imag = round_both(norm_scale * (product('qh,hkc->qkc', cos_lat, lon_imag) - product('qh,hkc->qkc', sin_lat, lon_real)))
    freq_real = freq_real.reshape(height, breadth, blocks, block_size)
    freq_imag = freq_imag.reshape(height, breadth, blocks, block_size)
    pre_real, pre_imag = complex_mix(freq_real, freq_imag, inner_weight, inner_bias)
    hid_real = low(smooth_gelu(low_back(pre_real)))
    hid_imag = low(smooth_gelu(low_back(pre_imag)))
    out_real, out_imag = complex_mix(hid_real, hid_imag, outer_weight, outer_bias)
    spec_real = low(shrink(low_back(out_real))).reshape(height, breadth, channels)
    spec_imag = low(shrink(low_back(out_imag))).reshape(height, breadth, channels)
    back_real = round_both(norm_scale * (product('hq,qkc->hkc', cos_lat, spec_real) - product('hq,qkc->hkc', sin_lat, spec_imag)))
    back_imag = round_both(norm_scale * (product('hq,qkc->hkc', cos_lat, spec_imag) + product('hq,qkc->hkc', sin_lat, spec_real)))
    filtered = low_back(product('hkc,kw->hwc', back_real, cos_lon) - product('hkc,kw->hwc', back_imag, sin_lon))
    mixed_field = filtered + normed + inside
    second = low(layer_norm(mixed_field, second_gain, second_shift))
    preact = low_back(product('hwc,fc->hwf', second, hidden_weight) + hidden_bias)
    hidden_act = low(smooth_gelu(preact))
    branch = low_back(product('hwf,fc->hwc', hidden_act, output_weight) + output_bias)
    return (mixed_field + branch) * inside_mask

def reference(frames, regions, cotangent, first_gain, first_shift, inner_weight, inner_bias, outer_weight, outer_bias, second_gain, second_shift, hidden_weight, hidden_bias, output_weight, output_bias):
    height = frames.shape[1]
    breadth = frames.shape[2]
    cos_lon, sin_lon = tables(breadth, breadth)
    cos_lat, sin_lat = tables(H, height)
    weights = tuple((weight.astype(jnp.float32) for weight in (first_gain, first_shift, inner_weight, inner_bias, outer_weight, outer_bias, second_gain, second_shift, hidden_weight, hidden_bias, output_weight, output_bias)))

    def forward(field, params):

        def single(pair):
            return frame_forward(pair[0], pair[1], params, cos_lon, sin_lon, cos_lat, sin_lat)
        return lax.map(jax.checkpoint(single), (field, regions))
    output, pullback = jax.vjp(forward, frames.astype(jnp.float32), weights)
    field_grad, param_grads = pullback(cotangent.astype(jnp.float32))
    return (output.astype(jnp.bfloat16), field_grad.astype(jnp.bfloat16), param_grads[0], param_grads[1], param_grads[2], param_grads[3], param_grads[4], param_grads[5], param_grads[6], param_grads[7], param_grads[8], param_grads[9], param_grads[10], param_grads[11])
```

```python
import functools
import math

import jax
import jax.numpy as jnp
import numpy as np
from jax import lax
from jax.experimental import pallas as pl
from jax.experimental.pallas import tpu as pltpu
from jax.sharding import PartitionSpec as P

H = 90
LANES = 128
GROUP = 4
KSTEP = 4

epsilon = 1e-05
shrink_level = 0.01

f32 = jnp.float32
bf16 = jnp.bfloat16


class Plan:
    def __init__(self, micro, rows, cols, channels, blocks, lat, lon):
        self.micro, self.rows, self.cols, self.channels, self.blocks = micro, rows, cols, channels, blocks
        self.lat, self.lon = lat, lon
        self.size = channels // blocks
        self.groups = -(-rows // GROUP)
        self.used = self.groups * cols
        self.packed = -(-self.used // 16) * 16
        self.padcol = -(-cols // 16) * 16
        self.stage = self.groups * self.padcol
        self.window = -(-(cols + 15) // 16) * 16
        self.slots = lat * self.groups * GROUP
        self.height = rows * lat
        self.breadth = cols * lon
        self.lanes = GROUP * self.size
        self.scale = float(H * self.breadth) ** (-0.5)

    def window_start(self, g):
        return min(self.cols * g // 16 * 16, self.packed - self.window)


def angle_tables(count, total):
    index = np.arange(total)
    turns = (index[:, None] * index[None, :]) % count
    angle = turns * (2.0 * math.pi / count)
    keep = ((index[:, None] < count) & (index[None, :] < count)).astype(np.float64)
    return np.cos(angle) * keep, np.sin(angle) * keep


def lon_tables(plan):
    cos, sin = angle_tables(plan.breadth, plan.breadth)
    breadth, win = plan.breadth, plan.window
    out = np.zeros((plan.groups, 2 * breadth, plan.lon * win), np.float32)
    for g in range(plan.groups):
        offset = plan.cols * g - plan.window_start(g)
        for s in range(plan.lon):
            w = slice(s * plan.cols, (s + 1) * plan.cols)
            at = slice(s * win + offset, s * win + offset + plan.cols)
            out[g, :breadth, at] = cos[:, w]
            out[g, breadth:, at] = -sin[:, w]
    return out.astype(jnp.bfloat16), np.ascontiguousarray(out.transpose(0, 2, 1)).astype(jnp.bfloat16)


def lat_tables(plan):
    cos, sin = angle_tables(H, plan.height)
    n = plan.slots
    slot = np.array(
        [s * plan.groups * GROUP + r for s in range(plan.lat) for r in range(plan.rows)]
    )
    c = np.zeros((n, n))
    s = np.zeros((n, n))
    c[: plan.height, slot] = cos
    s[: plan.height, slot] = sin
    forward = np.block([[c, s], [-s, c]])
    inverse = np.block([[c.T, -s.T], [s.T, c.T]])
    return forward.astype(np.float32).astype(jnp.bfloat16), inverse.astype(np.float32).astype(jnp.bfloat16)


def pack_table(plan):
    out = np.zeros((plan.packed, plan.stage), np.float32)
    for g in range(plan.groups):
        for j in range(plan.cols):
            out[plan.cols * g + j, plan.padcol * g + j] = 1.0
    return out.astype(jnp.bfloat16), np.ascontiguousarray(out.T).astype(jnp.bfloat16)


def dot(a, b):
    return lax.dot_general(a, b, (((1,), (0,)), ((), ())), preferred_element_type=f32)


def dot_nt(a, b):
    return lax.dot_general(a, b, (((1,), (1,)), ((), ())), preferred_element_type=f32)


def dot_tn(a, b):
    return lax.dot_general(a, b, (((0,), (0,)), ((), ())), preferred_element_type=f32)


def gelu_pair(x):
    phi = 0.5 + 0.5 * lax.erf(x * (0.5**0.5))
    density = jnp.exp(-0.5 * x * x) * (1.0 / math.sqrt(2.0 * math.pi))
    return x * phi, phi + x * density


def full(shape):
    return pl.BlockSpec(shape, lambda *_: (0,) * len(shape), pipeline_mode=pl.Buffered(1))


def params(mib):
    return pltpu.CompilerParams(vmem_limit_bytes=mib * 2**20)


def token_mask(plan, meta_ref, frame, i):
    p = lax.broadcasted_iota(jnp.int32, (plan.packed, 1), 0)
    g = jnp.zeros_like(p)
    for t in range(1, plan.groups):
        g += (p >= plan.cols * t).astype(jnp.int32)
    j = p - plan.cols * g
    r = GROUP * g + i
    h = meta_ref[frame, 4] + r
    w = meta_ref[frame, 5] + j
    d = w - meta_ref[frame, 2]
    d = jnp.where(d < 0, d + plan.breadth, d)
    inside = (
        (r < plan.rows)
        & (p < plan.used)
        & (h >= meta_ref[frame, 0])
        & (h < meta_ref[frame, 0] + meta_ref[frame, 1])
        & (d < meta_ref[frame, 3])
    )
    return inside.astype(f32)


def load_tile(plan, ref, stage_ref, pack_ref, i):
    for g in range(plan.groups):
        r = GROUP * g + i
        at = slice(plan.padcol * g, plan.padcol * g + plan.cols)

        @pl.when(r < plan.rows)
        def _():
            stage_ref[at, :] = ref[0, r]

    return dot(pack_ref[...], stage_ref[...])


def store_tile(plan, ref, value, unpack_ref, i):
    spread = dot(unpack_ref[...], value).astype(bf16)
    for g in range(plan.groups):
        r = GROUP * g + i

        @pl.when(r < plan.rows)
        def _():
            ref[0, r] = spread[plan.padcol * g : plan.padcol * g + plan.cols]


def statistics(x):
    centre = jnp.mean(x, axis=-1, keepdims=True)
    centred = x - centre
    spread = jnp.mean(centred * centred, axis=-1, keepdims=True)
    r = lax.rsqrt(spread + epsilon)
    return centred * r, r


def norm_back(g, xhat, r):
    return r * (g - jnp.mean(g, axis=-1, keepdims=True) - xhat * jnp.mean(g * xhat, axis=-1, keepdims=True))


def join_blocks(plan, ref, i):
    at = slice(i * plan.size, (i + 1) * plan.size)
    return jnp.concatenate([ref[b, :, at] for b in range(plan.blocks)], axis=1)


def split_blocks(plan, ref, values):
    for b in range(plan.blocks):
        at = slice(b * plan.size, (b + 1) * plan.size)
        ref[b] = jnp.concatenate([v[:, at] for v in values], axis=1)


def first_kernel(plan, meta_ref, frames_ref, pack_ref, gain_ref, shift_ref, send_ref, stage_ref):
    frame = pl.program_id(0)
    stage_ref[...] = jnp.zeros_like(stage_ref)
    values = []
    for i in range(GROUP):
        if GROUP * (plan.groups - 1) + i >= plan.rows:
            stage_ref[plan.padcol * (plan.groups - 1) :, :] = jnp.zeros(
                (plan.padcol, plan.channels), bf16
            )
        inside = load_tile(plan, frames_ref, stage_ref, pack_ref, i) * token_mask(plan, meta_ref, frame, i)
        xhat, _ = statistics(inside)
        values.append((xhat * gain_ref[...] + shift_ref[...]).astype(bf16))
    split_blocks(plan, send_ref, values)


def first_call(plan, meta, frames, pack, gain, shift):
    tile = (1, plan.rows, plan.cols, plan.channels)
    return pl.pallas_call(
        functools.partial(first_kernel, plan),
        grid=(plan.micro,),
        in_specs=[
            pl.BlockSpec(memory_space=pltpu.SMEM),
            pl.BlockSpec(tile, lambda f: (f, 0, 0, 0)),
            full(pack.shape),
            full(gain.shape),
            full(shift.shape),
        ],
        out_specs=pl.BlockSpec((plan.blocks, plan.packed, plan.lanes), lambda f: (f, 0, 0)),
        out_shape=jax.ShapeDtypeStruct((plan.micro * plan.blocks, plan.packed, plan.lanes), bf16),
        scratch_shapes=[pltpu.VMEM((plan.stage, plan.channels), bf16)],
        compiler_params=params(48),
    )(meta, frames, pack, gain, shift)


def spectral_kernel(plan, middle, streams_in, streams_out, sums, *refs):
    (recv_ref, lon_ref, lon_back_ref, lat_ref, lat_back_ref, w_in_ref, w_out_ref, b_in_ref, b_out_ref), refs = (
        refs[:9],
        refs[9:],
    )
    ins, refs = refs[:streams_in], refs[streams_in:]
    send_ref, refs = refs[0], refs[1:]
    outs, refs = refs[:streams_out], refs[streams_out:]
    totals, refs = refs[:sums], refs[sums:]
    wide_ref, tall_ref = refs
    step = pl.program_id(0)
    groups, slots, breadth, win, size = plan.groups, plan.slots, plan.breadth, plan.window, plan.size
    kinds = 2 * breadth
    middle_steps = breadth // KSTEP

    def window_start(g):
        return pl.multiple_of(
            jnp.minimum(plan.cols * g // 16 * 16, plan.packed - win), 16
        )

    @pl.when(step == 0)
    def _():
        send_ref[...] = jnp.zeros_like(send_ref)
        for total in totals:
            total[...] = jnp.zeros_like(total)

    @pl.when(step < groups)
    def _():
        g = step
        ws = window_start(g)
        table = lon_ref[g]
        for lat in range(plan.lat):
            rows = jnp.concatenate(
                [recv_ref[lon * plan.lat + lat, pl.ds(ws, win), :] for lon in range(plan.lon)], axis=0
            )
            pad = jnp.zeros((plan.lon * win, LANES - size), bf16)
            for pair in range(GROUP // 2):
                pieces = []
                for i in (2 * pair, 2 * pair + 1):
                    pieces += [rows[:, i * size : (i + 1) * size], pad]
                out = dot(table, jnp.concatenate(pieces, axis=1)).astype(bf16).astype(f32)
                for n in range(2):
                    slot = lat * groups * GROUP + GROUP * g + 2 * pair + n
                    wide_ref[pl.ds(slot, kinds, stride=slots), :] = out[:, n * LANES : (n + 1) * LANES]

    @pl.when((step >= groups) & (step < groups + middle_steps))
    def _():
        first = (step - groups) * KSTEP
        spectra = []
        for pair in range(KSTEP // 2):
            columns = []
            for n in range(2):
                k = first + 2 * pair + n
                columns.append(
                    jnp.concatenate(
                        [
                            wide_ref[pl.ds(pl.multiple_of(k * slots, 8), slots), :],
                            wide_ref[pl.ds(pl.multiple_of((breadth + k) * slots, 8), slots), :],
                        ],
                        axis=0,
                    ).astype(bf16)
                )
            out = dot(lat_ref[...], jnp.concatenate(columns, axis=1)) * plan.scale
            for n in range(2):
                at = slice(n * LANES, (n + 1) * LANES)
                spectra.append(jnp.concatenate([out[:slots, at], out[slots:, at]], axis=1))
        result = middle(
            jnp.concatenate(spectra, axis=0), w_in_ref, w_out_ref, b_in_ref, b_out_ref, ins, outs, totals
        )
        for pair in range(KSTEP // 2):
            columns = []
            for n in range(2):
                at = slice((2 * pair + n) * slots, (2 * pair + n + 1) * slots)
                columns.append(jnp.concatenate([result[at, :LANES], result[at, LANES:]], axis=0))
            out = dot(lat_back_ref[...], jnp.concatenate(columns, axis=1)) * plan.scale
            out = out.astype(bf16).astype(f32)
            for n in range(2):
                k = first + 2 * pair + n
                at = slice(n * LANES, (n + 1) * LANES)
                tall_ref[pl.ds(k, slots, stride=kinds), :] = out[:slots, at]
                tall_ref[pl.ds(breadth + k, slots, stride=kinds), :] = out[slots:, at]

    @pl.when(step >= groups + middle_steps)
    def _():
        g = step - (groups + middle_steps)
        ws = window_start(g)
        table = lon_back_ref[g]
        for lat in range(plan.lat):
            pieces = []
            for pair in range(GROUP // 2):
                columns = []
                for i in (2 * pair, 2 * pair + 1):
                    slot = lat * groups * GROUP + GROUP * g + i
                    columns.append(tall_ref[pl.ds(pl.multiple_of(slot * kinds, 8), kinds), :].astype(bf16))
                out = dot(table, jnp.concatenate(columns, axis=1)).astype(bf16)
                pieces += [out[:, :size], out[:, LANES : LANES + size]]
            out = jnp.concatenate(pieces, axis=1)
            for lon in range(plan.lon):
                send_ref[lon * plan.lat + lat, pl.ds(ws, win), :] += out[lon * win : (lon + 1) * win]


def forward_middle(freq, w_in_ref, w_out_ref, b_in_ref, b_out_ref, ins, outs, totals):
    freq_ref, hid_ref, slope_ref = outs
    freq = freq.astype(bf16)
    freq_ref[...] = freq
    hid, slope = gelu_pair(dot(freq, w_in_ref[...]) + b_in_ref[...])
    hid = hid.astype(bf16)
    hid_ref[...] = hid
    slope_ref[...] = slope
    out = dot(hid, w_out_ref[...]) + b_out_ref[...]
    return (out - shrink_level * out * lax.rsqrt(out * out + shrink_level * shrink_level)).astype(bf16)


def backward_middle(grad_spec, w_in_ref, w_out_ref, b_in_ref, b_out_ref, ins, outs, totals):
    freq_ref, hid_ref, slope_ref = ins
    in_sum_ref, out_sum_ref, in_bias_ref, out_bias_ref = totals
    hid = hid_ref[...]
    out = dot(hid, w_out_ref[...]) + b_out_ref[...]
    r = lax.rsqrt(out * out + shrink_level * shrink_level)
    grad_out = (grad_spec * (1.0 - shrink_level**3 * (r * r * r))).astype(bf16)
    out_sum_ref[...] += dot_tn(hid, grad_out)
    out_bias_ref[...] += jnp.sum(grad_out.astype(f32), axis=0, keepdims=True)
    grad_pre = (dot_nt(grad_out, w_out_ref[...]) * slope_ref[...]).astype(bf16)
    in_sum_ref[...] += dot_tn(freq_ref[...], grad_pre)
    in_bias_ref[...] += jnp.sum(grad_pre.astype(f32), axis=0, keepdims=True)
    return dot_nt(grad_pre, w_in_ref[...]).astype(bf16)


def spectral_call(plan, middle, recv, tables, weights, streams_in, out_types, sums):
    middle_steps = plan.breadth // KSTEP
    rows = KSTEP * plan.slots
    consts = (recv,) + tables + weights
    stream = pl.BlockSpec((rows, 2 * LANES), lambda s: (jnp.clip(s - plan.groups, 0, middle_steps - 1), 0))
    sum_shapes = (
        [(2 * LANES, 2 * LANES)] * 2 + [(1, 2 * LANES)] * 2 if sums else []
    )
    total_rows = plan.breadth * plan.slots
    return pl.pallas_call(
        functools.partial(spectral_kernel, plan, middle, len(streams_in), len(out_types), len(sum_shapes)),
        grid=(plan.groups * 2 + middle_steps,),
        in_specs=[full(c.shape) for c in consts] + [stream] * len(streams_in),
        out_specs=[full(recv.shape)] + [stream] * len(out_types) + [full(s) for s in sum_shapes],
        out_shape=[jax.ShapeDtypeStruct(recv.shape, bf16)]
        + [jax.ShapeDtypeStruct((total_rows, 2 * LANES), t) for t in out_types]
        + [jax.ShapeDtypeStruct(s, f32) for s in sum_shapes],
        scratch_shapes=[
            pltpu.VMEM((2 * plan.breadth * plan.slots, LANES), f32),
            pltpu.VMEM((2 * plan.breadth * plan.slots, LANES), f32),
        ],
        compiler_params=params(60),
    )(*consts, *streams_in)


def block_matrix(plan, weight):
    pad = ((0, LANES - plan.size), (0, LANES - plan.size))
    real = jnp.pad(weight[0], pad)
    imag = jnp.pad(weight[1], pad)
    return jnp.concatenate(
        [jnp.concatenate([real, imag], axis=1), jnp.concatenate([-imag, real], axis=1)], axis=0
    )


def block_bias(plan, bias):
    return jnp.pad(bias.astype(f32), ((0, 0), (0, LANES - plan.size))).reshape(1, 2 * LANES)


FCHUNK = 512


def ffn_kernel(
    plan,
    hidden,
    meta_ref,
    frames_ref,
    cot_ref,
    recv_ref,
    pack_ref,
    unpack_ref,
    gain_one_ref,
    shift_one_ref,
    gain_two_ref,
    shift_two_ref,
    w_hidden_ref,
    b_hidden_ref,
    w_out_ref,
    b_out_ref,
    mixed_ref,
    send_ref,
    grad_mixed_ref,
    second_ref,
    branch_grad_ref,
    hid_ref,
    pre_grad_ref,
    gain_sum_ref,
    shift_sum_ref,
    out_bias_sum_ref,
    hidden_bias_sum_ref,
    stage_ref,
    filt_ref,
    keep_ref,
    branch_ref,
    grad_ref,
):
    frame, i = pl.program_id(0), pl.program_id(1)

    @pl.when((frame == 0) & (i == 0))
    def _():
        stage_ref[...] = jnp.zeros_like(stage_ref)
        for ref in (gain_sum_ref, shift_sum_ref, out_bias_sum_ref, hidden_bias_sum_ref):
            ref[...] = jnp.zeros_like(ref)

    @pl.when(i == 0)
    def _():
        for n in range(GROUP):
            filt_ref[n] = join_blocks(plan, recv_ref, n)

    mask = token_mask(plan, meta_ref, frame, i)
    inside = load_tile(plan, frames_ref, stage_ref, pack_ref, i) * mask
    xhat_one, _ = statistics(inside)
    normed = xhat_one * gain_one_ref[...] + shift_one_ref[...]
    mixed = filt_ref[i].astype(f32) + normed + inside
    xhat, r = statistics(mixed)
    second = (xhat * gain_two_ref[...] + shift_two_ref[...]).astype(bf16)
    second_ref[0] = second
    grad_out = load_tile(plan, cot_ref, stage_ref, pack_ref, i) * mask
    grad_branch = grad_out.astype(bf16)
    branch_grad_ref[0] = grad_branch
    out_bias_sum_ref[...] += jnp.sum(grad_branch.astype(f32), axis=0, keepdims=True)
    branch_ref[...] = jnp.zeros_like(branch_ref)
    grad_ref[...] = jnp.zeros_like(grad_ref)
    for c in range(hidden // FCHUNK):
        at = slice(c * FCHUNK, (c + 1) * FCHUNK)
        w_hidden = w_hidden_ref[at, :]
        w_out = w_out_ref[at, :]
        hid, slope = gelu_pair(dot_nt(second, w_hidden) + b_hidden_ref[:, at])
        hid = hid.astype(bf16)
        hid_ref[0, :, at] = hid
        branch_ref[...] += dot(hid, w_out)
        grad_pre = (dot_nt(grad_branch, w_out) * slope).astype(bf16)
        pre_grad_ref[0, :, at] = grad_pre
        hidden_bias_sum_ref[:, at] += jnp.sum(grad_pre.astype(f32), axis=0, keepdims=True)
        grad_ref[...] += dot(grad_pre, w_hidden)
    store_tile(
        plan, mixed_ref, ((mixed + branch_ref[...] + b_out_ref[...]) * mask).astype(bf16), unpack_ref, i
    )
    grad_second = grad_ref[...]
    gain_sum_ref[...] += jnp.sum(grad_second * xhat, axis=0, keepdims=True)
    shift_sum_ref[...] += jnp.sum(grad_second, axis=0, keepdims=True)
    grad_mixed = grad_out + norm_back(grad_second * gain_two_ref[...], xhat, r)
    grad_mixed_ref[0, 0] = grad_mixed
    keep_ref[i] = grad_mixed.astype(bf16)

    @pl.when(i == GROUP - 1)
    def _():
        split_blocks(plan, send_ref, [keep_ref[n] for n in range(GROUP)])


def ffn_call(plan, meta, frames, cot, recv, consts):
    hidden = consts[6].shape[0]
    tile = pl.BlockSpec((1, plan.rows, plan.cols, plan.channels), lambda f, i: (f, 0, 0, 0))
    packet = pl.BlockSpec((plan.blocks, plan.packed, plan.lanes), lambda f, i: (f, 0, 0))
    token = pl.BlockSpec((1, plan.packed, plan.channels), lambda f, i: (f * GROUP + i, 0, 0))
    wide = pl.BlockSpec((1, plan.packed, hidden), lambda f, i: (f * GROUP + i, 0, 0))
    tiles = plan.micro * GROUP
    sums = [(1, plan.channels)] * 3 + [(1, hidden)]
    return pl.pallas_call(
        functools.partial(ffn_kernel, plan, hidden),
        grid=(plan.micro, GROUP),
        in_specs=[pl.BlockSpec(memory_space=pltpu.SMEM), tile, tile, packet] + [full(c.shape) for c in consts],
        out_specs=[
            tile,
            packet,
            pl.BlockSpec((1, 1, plan.packed, plan.channels), lambda f, i: (f, i, 0, 0)),
            token,
            token,
            wide,
            wide,
        ]
        + [full(s) for s in sums],
        out_shape=[
            jax.ShapeDtypeStruct(frames.shape, bf16),
            jax.ShapeDtypeStruct(recv.shape, bf16),
            jax.ShapeDtypeStruct((plan.micro, GROUP, plan.packed, plan.channels), f32),
            jax.ShapeDtypeStruct((tiles, plan.packed, plan.channels), bf16),
            jax.ShapeDtypeStruct((tiles, plan.packed, plan.channels), bf16),
            jax.ShapeDtypeStruct((tiles, plan.packed, hidden), bf16),
            jax.ShapeDtypeStruct((tiles, plan.packed, hidden), bf16),
        ]
        + [jax.ShapeDtypeStruct(s, f32) for s in sums],
        scratch_shapes=[
            pltpu.VMEM((plan.stage, plan.channels), bf16),
            pltpu.VMEM((GROUP, plan.packed, plan.channels), bf16),
            pltpu.VMEM((GROUP, plan.packed, plan.channels), bf16),
            pltpu.VMEM((plan.packed, plan.channels), f32),
            pltpu.VMEM((plan.packed, plan.channels), f32),
        ],
        compiler_params=params(60),
    )(meta, frames, cot, recv, *consts)


def last_kernel(
    plan,
    meta_ref,
    frames_ref,
    recv_ref,
    grad_mixed_ref,
    pack_ref,
    unpack_ref,
    gain_ref,
    out_ref,
    gain_sum_ref,
    shift_sum_ref,
    stage_ref,
):
    frame = pl.program_id(0)

    @pl.when(frame == 0)
    def _():
        gain_sum_ref[...] = jnp.zeros_like(gain_sum_ref)
        shift_sum_ref[...] = jnp.zeros_like(shift_sum_ref)

    stage_ref[...] = jnp.zeros_like(stage_ref)
    for i in range(GROUP):
        mask = token_mask(plan, meta_ref, frame, i)
        inside = load_tile(plan, frames_ref, stage_ref, pack_ref, i) * mask
        xhat, r = statistics(inside)
        grad_mixed = grad_mixed_ref[0, i]
        grad_normed = join_blocks(plan, recv_ref, i).astype(f32) + grad_mixed
        gain_sum_ref[...] += jnp.sum(grad_normed * xhat, axis=0, keepdims=True)
        shift_sum_ref[...] += jnp.sum(grad_normed, axis=0, keepdims=True)
        grad_inside = grad_mixed + norm_back(grad_normed * gain_ref[...], xhat, r)
        store_tile(plan, out_ref, (grad_inside * mask).astype(bf16), unpack_ref, i)


def last_call(plan, meta, frames, recv, grad_mixed, consts):
    tile = pl.BlockSpec((1, plan.rows, plan.cols, plan.channels), lambda f: (f, 0, 0, 0))
    return pl.pallas_call(
        functools.partial(last_kernel, plan),
        grid=(plan.micro,),
        in_specs=[
            pl.BlockSpec(memory_space=pltpu.SMEM),
            tile,
            pl.BlockSpec((plan.blocks, plan.packed, plan.lanes), lambda f: (f, 0, 0)),
            pl.BlockSpec((1, GROUP, plan.packed, plan.channels), lambda f: (f, 0, 0, 0)),
        ]
        + [full(c.shape) for c in consts],
        out_specs=[tile, full((1, plan.channels)), full((1, plan.channels))],
        out_shape=[
            jax.ShapeDtypeStruct(frames.shape, bf16),
            jax.ShapeDtypeStruct((1, plan.channels), f32),
            jax.ShapeDtypeStruct((1, plan.channels), f32),
        ],
        scratch_shapes=[pltpu.VMEM((plan.stage, plan.channels), bf16)],
        compiler_params=params(56),
    )(meta, frames, recv, grad_mixed, *consts)


AXES = ("dp", "lon", "lat")


def exchange(values):
    return lax.all_to_all(values, ("lon", "lat"), 0, 0, tiled=True)


def reduce_over(values, axis):
    moved = lax.all_to_all(values.astype(bf16), axis, 0, 0, tiled=True)
    return jnp.sum(moved.astype(f32), axis=0)


def body(
    frames,
    regions,
    cotangent,
    first_gain,
    first_shift,
    inner_weight,
    inner_bias,
    outer_weight,
    outer_bias,
    second_gain,
    second_shift,
    hidden_weight,
    hidden_bias,
    output_weight,
    output_bias,
):
    dp, lon, lat = (lax.axis_size(a) for a in AXES)
    lon_place, lat_place = lax.axis_index("lon"), lax.axis_index("lat")
    micro, rows, cols, channels = frames.shape
    blocks = inner_weight.shape[0]
    plan = Plan(micro, rows, cols, channels, blocks, lat, lon)
    place = lon_place * lat + lat_place
    own_block = place % blocks
    hidden_rows = hidden_weight.shape[0]
    hidden = hidden_rows * dp * lon * lat

    origin = jnp.stack([lat_place * rows, lon_place * cols]).astype(jnp.int32)
    meta = jnp.concatenate([regions, jnp.broadcast_to(origin, (micro, 2))], axis=1)
    pack, unpack = (jnp.asarray(t) for t in pack_table(plan))
    tables = tuple(jnp.asarray(t) for t in lon_tables(plan) + lat_tables(plan))

    def row(v):
        return v.astype(f32).reshape(1, -1)

    def own(v):
        return lax.dynamic_index_in_dim(v, own_block, 0, keepdims=False)

    spectral_weights = (
        block_matrix(plan, own(inner_weight)),
        block_matrix(plan, own(outer_weight)),
        block_bias(plan, own(inner_bias)),
        block_bias(plan, own(outer_bias)),
    )

    bias_row = jnp.pad(hidden_bias.reshape(1, hidden_rows), ((0, 7), (0, channels - hidden_rows)))
    gathered = lax.all_gather(
        jnp.concatenate([hidden_weight, output_weight, bias_row], axis=0), AXES, axis=0
    )
    w_hidden = gathered[:, :hidden_rows].reshape(hidden, channels)
    w_output = gathered[:, hidden_rows : 2 * hidden_rows].reshape(hidden, channels)
    b_hidden = gathered[:, 2 * hidden_rows, :hidden_rows].astype(f32).reshape(1, hidden)

    send = first_call(plan, meta, frames, pack, row(first_gain), row(first_shift))
    send, freq, hid, slope = spectral_call(
        plan, forward_middle, exchange(send), tables, spectral_weights, (), (bf16, bf16, f32), False
    )
    (
        mixed_frames,
        send,
        grad_mixed,
        second,
        grad_branch,
        hidden_act,
        grad_preact,
        second_gain_sum,
        second_shift_sum,
        output_bias_sum,
        hidden_bias_sum,
    ) = ffn_call(
        plan,
        meta,
        frames,
        cotangent,
        exchange(send),
        (
            pack,
            unpack,
            row(first_gain),
            row(first_shift),
            row(second_gain),
            row(second_shift),
            w_hidden,
            b_hidden,
            w_output,
            row(output_bias),
        ),
    )
    received = exchange(send)

    def weight_grad(left, right):
        return jnp.einsum("atf,atc->fc", left, right, preferred_element_type=f32)

    weight_sums = jnp.stack(
        [
            weight_grad(grad_preact, second).reshape(dp, lon, lat, hidden_rows, channels),
            weight_grad(hidden_act, grad_branch).reshape(dp, lon, lat, hidden_rows, channels),
        ],
        axis=3,
    )
    ffn_grads = reduce_over(reduce_over(reduce_over(weight_sums, "dp"), "lon"), "lat")

    send, inner_sum, outer_sum, inner_bias_sum, outer_bias_sum = spectral_call(
        plan, backward_middle, received, tables, spectral_weights, (freq, hid, slope), (), True
    )
    frame_grad, first_gain_sum, first_shift_sum = last_call(
        plan, meta, frames, exchange(send), grad_mixed, (pack, unpack, row(first_gain))
    )

    def spread(value):
        return lax.dynamic_update_slice_in_dim(
            jnp.zeros((blocks,) + value.shape, f32), value[None], own_block, 0
        )

    def complex_sum(full_sum):
        s = plan.size
        rr, ri = full_sum[:s, :s], full_sum[:s, LANES : LANES + s]
        ir, ii = full_sum[LANES : LANES + s, :s], full_sum[LANES : LANES + s, LANES : LANES + s]
        return spread(jnp.stack([rr + ii, ri - ir]))

    def bias_sum(full_sum):
        return spread(full_sum.reshape(2, LANES)[:, : plan.size])

    sums = lax.psum(
        (
            first_gain_sum,
            first_shift_sum,
            complex_sum(inner_sum),
            bias_sum(inner_bias_sum),
            complex_sum(outer_sum),
            bias_sum(outer_bias_sum),
            second_gain_sum,
            second_shift_sum,
            hidden_bias_sum,
            output_bias_sum,
        ),
        AXES,
    )
    order = lax.axis_index(AXES)
    hidden_bias_grad = lax.dynamic_slice_in_dim(sums[8].reshape(hidden), order * hidden_rows, hidden_rows, 0)
    flat = lambda v: v.reshape(channels)
    return (
        mixed_frames,
        frame_grad,
        flat(sums[0]),
        flat(sums[1]),
        sums[2],
        sums[3],
        sums[4],
        sums[5],
        flat(sums[6]),
        flat(sums[7]),
        ffn_grads[0],
        hidden_bias_grad,
        ffn_grads[1],
        flat(sums[9]),
    )


def solution(mesh):
    field = P("dp", "lat", "lon", None)
    rows = P(AXES, None)
    return jax.shard_map(
        body,
        mesh=mesh,
        in_specs=(field, P("dp", None), field) + (P(),) * 8 + (rows, P(AXES), rows, P()),
        out_specs=(field, field) + (P(),) * 8 + (rows, P(AXES), rows, P()),
        check_vma=False,
    )
```

```python
import functools
import math

import jax
import jax.numpy as jnp
import numpy as np
from jax import lax
from jax.experimental import pallas as pl
from jax.experimental.pallas import tpu as pltpu
from jax.sharding import PartitionSpec as P

H = 90
LANES = 128
GROUP = 4
HALVES = 2
MAX_KSTEP = 12
HINT = 0.05

epsilon = 1e-05
shrink_level = 0.01

f32 = jnp.float32
bf16 = jnp.bfloat16


class Plan:
    def __init__(self, micro, rows, cols, channels, blocks, lat, lon):
        self.micro, self.rows, self.cols, self.channels, self.blocks = micro, rows, cols, channels, blocks
        self.lat, self.lon = lat, lon
        self.places = lat * lon
        self.size = channels // blocks
        self.groups = -(-rows // (GROUP * HALVES))
        self.padcol = -(-cols // 16) * 16
        self.packed = self.groups * self.padcol
        self.part = self.groups * GROUP
        self.slots = lat * self.part
        self.pitch = odd_pitch(self.slots)
        self.height = rows * lat
        self.breadth = cols * lon
        self.waves = self.breadth // HALVES
        self.padwave = -(-self.waves // 16) * 16
        self.lanes = GROUP * self.size
        self.scale = float(H * self.breadth) ** (-0.5)
        self.kstep = max(k for k in range(2, MAX_KSTEP + 1, 2) if self.waves % k == 0)


def odd_pitch(rows):
    rows = -(-rows // 8) * 8
    return rows + 8 if rows % 16 == 0 else rows


def angle_tables(count, total):
    index = np.arange(total)
    turns = (index[:, None] * index[None, :]) % count
    angle = turns * (2.0 * math.pi / count)
    keep = ((index[:, None] < count) & (index[None, :] < count)).astype(np.float64)
    return np.cos(angle) * keep, np.sin(angle) * keep


def lon_tables(plan):
    cos, sin = angle_tables(plan.breadth, plan.breadth)
    width = plan.lon * plan.padcol
    out = np.zeros((2, plan.breadth, width), np.float32)
    for s in range(plan.lon):
        w = slice(s * plan.cols, (s + 1) * plan.cols)
        at = slice(s * plan.padcol, s * plan.padcol + plan.cols)
        out[0, :, at] = cos[:, w]
        out[1, :, at] = -sin[:, w]
    back = np.zeros((2, width, 2, 2, plan.padwave), np.float32)
    for d in range(2):
        for n in range(2):
            half = (d + n) % 2
            waves = slice(half * plan.waves, (half + 1) * plan.waves)
            for kind in range(2):
                back[d, :, n, kind, : plan.waves] = out[kind, waves].T
    return out.reshape(2 * plan.breadth, width).astype(jnp.bfloat16), back.reshape(2, width, -1).astype(jnp.bfloat16)


def lat_tables(plan):
    cos, sin = angle_tables(H, plan.height)
    n = HALVES * plan.slots
    forward, inverse = [], []
    for d in range(2):
        c = np.zeros((n, n))
        s = np.zeros((n, n))
        for order in range(2):
            half = (d + order) % 2
            for lat in range(plan.lat):
                for r in range(plan.part):
                    row = half * plan.part + r
                    if row < plan.rows:
                        at = order * plan.slots + lat * plan.part + r
                        c[: plan.height, at] = cos[:, lat * plan.rows + row]
                        s[: plan.height, at] = sin[:, lat * plan.rows + row]
        forward.append(np.block([[c, s], [-s, c]]))
        inverse.append(np.block([[c.T, -s.T], [s.T, c.T]]))
    return tuple(np.stack(t).astype(np.float32).astype(jnp.bfloat16) for t in (forward, inverse))


def dot(a, b):
    return lax.dot_general(a, b, (((1,), (0,)), ((), ())), preferred_element_type=f32)


def dot_nt(a, b):
    return lax.dot_general(a, b, (((1,), (1,)), ((), ())), preferred_element_type=f32)


def dot_tn(a, b):
    return lax.dot_general(a, b, (((0,), (0,)), ((), ())), preferred_element_type=f32)


def gelu_pair(x):
    phi = 0.5 + 0.5 * lax.erf(x * (0.5**0.5))
    density = jnp.exp(-0.5 * x * x) * (1.0 / math.sqrt(2.0 * math.pi))
    return x * phi, phi + x * density


def full(shape):
    return pl.BlockSpec(shape, lambda *_: (0,) * len(shape), pipeline_mode=pl.Buffered(1))


def params(mib):
    return pltpu.CompilerParams(vmem_limit_bytes=mib * 2**20)


def cost(flops, moved):
    return pl.CostEstimate(flops=int(flops * HINT), bytes_accessed=int(moved * HINT), transcendentals=0)


def bump(ref, value):
    ref[...] += jnp.sum(value, axis=0, keepdims=True)


def row_mask(plan, meta_ref, half, i):
    p = lax.broadcasted_iota(jnp.int32, (plan.packed, 1), 0)
    g = jnp.zeros_like(p)
    for t in range(1, plan.groups):
        g += (p >= plan.padcol * t).astype(jnp.int32)
    j = p - plan.padcol * g
    r = plan.part * half + GROUP * g + i
    h = meta_ref[4] + r
    w = meta_ref[5] + j
    d = w - meta_ref[2]
    d = jnp.where(d < 0, d + plan.breadth, d)
    inside = (
        (r < plan.rows)
        & (j < plan.cols)
        & (h >= meta_ref[0])
        & (h < meta_ref[0] + meta_ref[1])
        & (d < meta_ref[3])
    )
    return inside.astype(f32)


def load_row(plan, ref, half, i):
    base = plan.part * half + i
    return jnp.concatenate([ref[0, base + GROUP * g] for g in range(plan.groups)], axis=0)


def store_row(plan, ref, value, half, i):
    base = plan.part * half + i
    for g in range(plan.groups):
        ref[base + GROUP * g] = value[plan.padcol * g : plan.padcol * (g + 1)]


def statistics(x):
    centre = jnp.mean(x, axis=-1, keepdims=True)
    centred = x - centre
    spread = jnp.mean(centred * centred, axis=-1, keepdims=True)
    r = lax.rsqrt(spread + epsilon)
    return centred * r, r


def norm_back(g, xhat, r):
    return r * (g - jnp.mean(g, axis=-1, keepdims=True) - xhat * jnp.mean(g * xhat, axis=-1, keepdims=True))


def join_blocks(plan, ref, first, i):
    at = slice(i * plan.size, (i + 1) * plan.size)
    return jnp.concatenate([ref[first + b, :, at] for b in range(plan.blocks)], axis=1)


def split_blocks(plan, ref, first, values):
    for b in range(plan.blocks):
        at = slice(b * plan.size, (b + 1) * plan.size)
        ref[first + b] = jnp.concatenate([v[:, at] for v in values], axis=1)


SCALARS = pl.BlockSpec(memory_space=pltpu.SMEM)


def tile_spec(plan, slot):
    return pl.BlockSpec(
        (1, HALVES * plan.part, plan.padcol, plan.channels),
        lambda *_: (slot, 0, 0, 0),
        pipeline_mode=pl.Buffered(1),
    )


def tile_shape(plan):
    return jax.ShapeDtypeStruct((HALVES * plan.part, plan.padcol, plan.channels), bf16)


def packet_shape(plan, count):
    return jax.ShapeDtypeStruct((count, plan.packed, plan.lanes), bf16)


def first_kernel(plan, meta_ref, frames_ref, gain_ref, shift_ref, send_ref, give_ref):
    d = meta_ref[6]
    for n, ref, first in ((0, send_ref, d * plan.blocks), (1, give_ref, 0)):
        half = d if n == 0 else 1 - d
        values = []
        for i in range(GROUP):
            inside = load_row(plan, frames_ref, half, i).astype(f32) * row_mask(plan, meta_ref, half, i)
            xhat, _ = statistics(inside)
            values.append((xhat * gain_ref[...] + shift_ref[...]).astype(bf16))
        split_blocks(plan, ref, first, values)


def first_call(plan, slot, meta, frames, gain, shift):
    shapes = [packet_shape(plan, plan.places), packet_shape(plan, plan.blocks)]
    return pl.pallas_call(
        functools.partial(first_kernel, plan),
        grid=(1,),
        in_specs=[SCALARS, tile_spec(plan, slot), full(gain.shape), full(shift.shape)],
        out_specs=[full(v.shape) for v in shapes],
        out_shape=shapes,
        compiler_params=params(32),
        cost_estimate=cost(5e9, 8e6),
    )(meta, frames, gain, shift)


def lon_kernel(plan, meta_ref, recv_ref, table_ref, keep_ref, give_ref, wide_ref):
    g = pl.program_id(0)
    kinds, size, pad = 2 * plan.breadth, plan.size, plan.padcol
    at = pl.ds(pl.multiple_of(g * pad, 16), pad)
    gap = jnp.zeros((plan.lon * pad, LANES - size), bf16)
    for lat in range(plan.lat):
        rows = jnp.concatenate([recv_ref[lon * plan.lat + lat, at, :] for lon in range(plan.lon)], axis=0)
        for pair in range(GROUP // 2):
            pieces = []
            for i in (2 * pair, 2 * pair + 1):
                pieces += [rows[:, i * size : (i + 1) * size], gap]
            out = dot(table_ref[...], jnp.concatenate(pieces, axis=1))
            for n in range(2):
                slot = lat * plan.part + GROUP * g + 2 * pair + n
                wide_ref[pl.ds(slot, kinds, stride=plan.pitch), :] = out[:, n * LANES : (n + 1) * LANES]

    @pl.when(g == plan.groups - 1)
    def _():
        d = meta_ref[6]
        for ref, half in ((keep_ref, d), (give_ref, 1 - d)):
            for kind in range(2):
                base = kind * plan.breadth + half * plan.waves

                def move(k, _, ref=ref, kind=kind, base=base):
                    row = pl.multiple_of((base + k) * plan.pitch, 8)
                    to = pl.multiple_of(k * plan.slots, 16)
                    ref[kind, pl.ds(to, plan.slots), :] = wide_ref[pl.ds(row, plan.slots), :].astype(bf16)
                    return _

                lax.fori_loop(0, plan.waves, move, 0, unroll=10)


def lon_call(plan, meta, recv, table):
    shape = jax.ShapeDtypeStruct((2, plan.waves * plan.slots, LANES), bf16)
    return pl.pallas_call(
        functools.partial(lon_kernel, plan),
        grid=(plan.groups,),
        in_specs=[SCALARS, full(recv.shape), full(table.shape)],
        out_specs=[full(shape.shape)] * 2,
        out_shape=[shape] * 2,
        scratch_shapes=[pltpu.VMEM((2 * plan.breadth * plan.pitch, LANES), f32)],
        compiler_params=params(40),
        cost_estimate=cost(4e9, 8e6),
    )(meta, recv, table)


def wave_kernel(plan, middle, counts, *refs):
    refs = list(refs)

    def take(n):
        got = tuple(refs[:n])
        del refs[:n]
        return got

    mine_ref, other_ref, lat_ref, lat_back_ref = take(4)
    weights = take(4)
    ins = take(counts[0])
    back_refs = take(2)
    outs = take(counts[1])
    totals = take(counts[2])
    tall_refs = refs[:2]
    sums_ref = totals[0] if totals else None
    totals = tuple(refs[2:])
    step = pl.program_id(0)
    slots, pitch = plan.slots, odd_pitch(2 * plan.padwave)
    both = HALVES * slots

    @pl.when(step == 0)
    def _():
        for ref in totals + tuple(tall_refs):
            ref[...] = jnp.zeros_like(ref)

    spectra = []
    for pair in range(plan.kstep // 2):
        columns = []
        for n in range(2):
            at = slice((2 * pair + n) * slots, (2 * pair + n + 1) * slots)
            columns.append(
                jnp.concatenate([ref[kind, at, :] for kind in range(2) for ref in (mine_ref, other_ref)], axis=0)
            )
        out = dot(lat_ref[...], jnp.concatenate(columns, axis=1)) * plan.scale
        for n in range(2):
            at = slice(n * LANES, (n + 1) * LANES)
            spectra.append(jnp.concatenate([out[:both, at], out[both:, at]], axis=1))
    result = middle(jnp.concatenate(spectra, axis=0), weights, ins, outs, totals)
    for pair in range(plan.kstep // 2):
        columns = []
        for n in range(2):
            at = slice((2 * pair + n) * both, (2 * pair + n + 1) * both)
            columns.append(jnp.concatenate([result[at, :LANES], result[at, LANES:]], axis=0))
        out = dot(lat_back_ref[...], jnp.concatenate(columns, axis=1)) * plan.scale
        for n in range(2):
            k = step * plan.kstep + 2 * pair + n
            at = slice(n * LANES, (n + 1) * LANES)
            for kind in range(2):
                for order in range(2):
                    low = kind * both + order * slots
                    tall_refs[order][pl.ds(kind * plan.padwave + k, slots, stride=pitch), :] = out[
                        low : low + slots, at
                    ]

    @pl.when(step == pl.num_programs(0) - 1)
    def _():
        for ref, tall_ref in zip(back_refs, tall_refs):

            def move(h, _, ref=ref, tall_ref=tall_ref):
                row = pl.multiple_of(h * pitch, 8)
                to = pl.multiple_of(h * 2 * plan.padwave, 16)
                ref[pl.ds(to, 2 * plan.padwave), :] = tall_ref[pl.ds(row, 2 * plan.padwave), :].astype(bf16)
                return _

            lax.fori_loop(0, slots, move, 0, unroll=4)

        if totals:
            size = plan.size
            low, high = slice(0, size), slice(LANES, LANES + size)
            for n, total in enumerate(totals[:2]):
                base = 2 * size * n
                sums_ref[base : base + size] = total[low, :LANES] + total[high, LANES:]
                sums_ref[base + size : base + 2 * size] = total[low, LANES:] - total[high, :LANES]
            rows = [total[:, at] for total in totals[2:] for at in (slice(0, LANES), slice(LANES, None))]
            rows.append(jnp.zeros((sums_ref.shape[0] - 4 * size - 4, LANES), f32))
            sums_ref[4 * size :] = jnp.concatenate(rows, axis=0)


def sum_rows(plan):
    return -(-(4 * plan.size + 4) // 16) * 16


def wave_call(plan, middle, mine, other, tables, weights, streams_in, out_types, sums):
    consts = tables + weights
    part = pl.BlockSpec((2, plan.kstep * plan.slots, LANES), lambda s: (0, s, 0))
    stream = pl.BlockSpec((plan.kstep * HALVES * plan.slots, 2 * LANES), lambda s: (s, 0))
    sum_shapes = [(sum_rows(plan), LANES)] if sums else []
    total_shapes = [(2 * LANES, 2 * LANES)] * 2 + [(1, 2 * LANES)] * 2 if sums else []
    back = jax.ShapeDtypeStruct((plan.slots * 2 * plan.padwave, LANES), bf16)
    rows = plan.waves * HALVES * plan.slots
    return pl.pallas_call(
        functools.partial(wave_kernel, plan, middle, (len(streams_in), len(out_types), len(sum_shapes))),
        grid=(plan.waves // plan.kstep,),
        in_specs=[part] * 2 + [full(c.shape) for c in consts] + [stream] * len(streams_in),
        out_specs=[full(back.shape)] * 2 + [stream] * len(out_types) + [full(s) for s in sum_shapes],
        out_shape=[back] * 2
        + [jax.ShapeDtypeStruct((rows, 2 * LANES), t) for t in out_types]
        + [jax.ShapeDtypeStruct(s, f32) for s in sum_shapes],
        scratch_shapes=[pltpu.VMEM((plan.slots * odd_pitch(2 * plan.padwave), LANES), f32)] * 2
        + [pltpu.VMEM(v, f32) for v in total_shapes],
        compiler_params=params(48),
        cost_estimate=cost(20e9, 24e6),
    )(mine, other, *consts, *streams_in)


def back_kernel(plan, summed, mine_ref, other_ref, table_ref, *refs):
    g = pl.program_id(0)
    held_ref = refs[0] if summed else None
    send_ref = refs[1 if summed else 0]
    totals = refs[2:] if summed else ()
    kinds, size, pad = 2 * plan.padwave, plan.size, plan.padcol
    rows = pl.ds(pl.multiple_of(g * pad, 16), pad)

    if summed:

        @pl.when(g == 0)
        def _():
            for total in totals:
                total[...] = jnp.zeros_like(total)

    for lat in range(plan.lat):
        pieces = []
        for pair in range(GROUP // 2):
            columns = []
            for i in (2 * pair, 2 * pair + 1):
                at = pl.ds(pl.multiple_of((lat * plan.part + GROUP * g + i) * kinds, 16), kinds)
                columns.append(jnp.concatenate([mine_ref[at, :], other_ref[at, :]], axis=0))
            out = dot(table_ref[...], jnp.concatenate(columns, axis=1)).astype(bf16)
            pieces += [out[:, :size], out[:, LANES : LANES + size]]
        out = jnp.concatenate(pieces, axis=1)
        for lon in range(plan.lon):
            source = lon * plan.lat + lat
            value = out[lon * pad : (lon + 1) * pad]
            send_ref[source, rows, :] = value
            if summed:
                value = value.astype(f32)
                bump(totals[0], value * held_ref[source, rows, :].astype(f32))
                bump(totals[1], value)


def back_call(plan, mine, other, table, held=None):
    consts = (mine, other, table) + (() if held is None else (held,))
    shapes = [packet_shape(plan, plan.places)]
    if held is not None:
        shapes += [jax.ShapeDtypeStruct((1, plan.lanes), f32)] * 2
    return pl.pallas_call(
        functools.partial(back_kernel, plan, held is not None),
        grid=(plan.groups,),
        in_specs=[full(c.shape) for c in consts],
        out_specs=[full(v.shape) for v in shapes],
        out_shape=shapes,
        compiler_params=params(32),
        cost_estimate=cost(4e9, 8e6),
    )(*consts)


def forward_middle(freq, weights, ins, outs, totals):
    w_in_ref, w_out_ref, b_in_ref, b_out_ref = weights
    freq_ref, hid_ref, slope_ref = outs
    freq = freq.astype(bf16)
    freq_ref[...] = freq
    hid, slope = gelu_pair(dot(freq, w_in_ref[...]) + b_in_ref[...])
    hid = hid.astype(bf16)
    hid_ref[...] = hid
    slope_ref[...] = slope.astype(slope_ref.dtype)
    out = dot(hid, w_out_ref[...]) + b_out_ref[...]
    return (out - shrink_level * out * lax.rsqrt(out * out + shrink_level * shrink_level)).astype(bf16)


def backward_middle(grad_spec, weights, ins, outs, totals):
    w_in_ref, w_out_ref, b_in_ref, b_out_ref = weights
    freq_ref, hid_ref, slope_ref = ins
    in_sum_ref, out_sum_ref, in_bias_ref, out_bias_ref = totals
    hid = hid_ref[...]
    out = dot(hid, w_out_ref[...]) + b_out_ref[...]
    r = lax.rsqrt(out * out + shrink_level * shrink_level)
    grad_out = (grad_spec * (1.0 - shrink_level**3 * (r * r * r))).astype(bf16)
    out_sum_ref[...] += dot_tn(hid, grad_out)
    bump(out_bias_ref, grad_out.astype(f32))
    grad_pre = (dot_nt(grad_out, w_out_ref[...]) * slope_ref[...].astype(f32)).astype(bf16)
    in_sum_ref[...] += dot_tn(freq_ref[...], grad_pre)
    bump(in_bias_ref, grad_pre.astype(f32))
    return dot_nt(grad_pre, w_in_ref[...]).astype(bf16)


def block_matrix(plan, weight):
    pad = ((0, LANES - plan.size), (0, LANES - plan.size))
    real = jnp.pad(weight[0], pad)
    imag = jnp.pad(weight[1], pad)
    return jnp.concatenate(
        [jnp.concatenate([real, imag], axis=1), jnp.concatenate([-imag, real], axis=1)], axis=0
    )


def block_bias(plan, bias):
    return jnp.pad(bias.astype(f32), ((0, 0), (0, LANES - plan.size))).reshape(1, 2 * LANES)


FCHUNK = 512
PAIR = 2


def ffn_kernel(plan, hidden, kept, *refs):
    (
        meta_ref,
        frames_ref,
        cot_ref,
        recv_ref,
        other_ref,
        gain_one_ref,
        shift_one_ref,
        gain_two_ref,
        shift_two_ref,
        b_hidden_ref,
        b_out_ref,
        *weight_refs,
    ) = refs[:15]
    (
        second_ref,
        branch_grad_ref,
        hid_ref,
        pre_grad_ref,
        mixed_ref,
        send_ref,
        give_ref,
        grad_mixed_ref,
        gain_sum_ref,
        shift_sum_ref,
        out_bias_sum_ref,
        gain_one_sum_ref,
        shift_one_sum_ref,
        hidden_bias_sum_ref,
        filt_ref,
        keep_ref,
        branch_ref,
        grad_ref,
    ) = refs[15 + kept :]
    order, pair = pl.program_id(0), pl.program_id(1)
    d = meta_ref[6]
    half = jnp.where(order == 0, d, 1 - d)
    rows = [PAIR * pair + n for n in range(PAIR)]

    @pl.when((order == 0) & (pair == 0))
    def _():
        for ref in (
            gain_sum_ref,
            shift_sum_ref,
            out_bias_sum_ref,
            gain_one_sum_ref,
            shift_one_sum_ref,
            hidden_bias_sum_ref,
        ):
            ref[...] = jnp.zeros_like(ref)

    @pl.when((order == 0) & (pair == 0))
    def _():
        for n in range(GROUP):
            filt_ref[n] = join_blocks(plan, recv_ref, d * plan.blocks, n)

    @pl.when((order == 1) & (pair == 0))
    def _():
        for n in range(GROUP):
            filt_ref[n] = join_blocks(plan, other_ref, 0, n)

    def tile(load):
        return jnp.concatenate([load(i) for i in rows], axis=0)

    mask = tile(lambda i: row_mask(plan, meta_ref, half, i))
    inside = tile(lambda i: load_row(plan, frames_ref, half, i)).astype(f32) * mask
    xhat_one, _ = statistics(inside)
    normed = xhat_one * gain_one_ref[...] + shift_one_ref[...]
    mixed = tile(lambda i: filt_ref[i]).astype(f32) + normed + inside
    xhat, r = statistics(mixed)
    second = (xhat * gain_two_ref[...] + shift_two_ref[...]).astype(bf16)
    second_ref[...] = second
    grad_out = tile(lambda i: load_row(plan, cot_ref, half, i)).astype(f32) * mask
    grad_branch = grad_out.astype(bf16)
    branch_grad_ref[...] = grad_branch
    bump(out_bias_sum_ref, grad_branch.astype(f32))
    for c in range(hidden // FCHUNK):
        at = slice(c * FCHUNK, (c + 1) * FCHUNK)
        which, low = divmod(c * FCHUNK, hidden // 2)
        w_hidden = weight_refs[which][low : low + FCHUNK, :]
        w_out = weight_refs[2 + which][low : low + FCHUNK, :]
        hid, slope = gelu_pair(dot_nt(second, w_hidden) + b_hidden_ref[:, at])
        hid = hid.astype(bf16)
        hid_ref[:, at] = hid
        grad_pre = (dot_nt(grad_branch, w_out) * slope).astype(bf16)
        pre_grad_ref[:, at] = grad_pre
        hidden_bias_sum_ref[:, at] += jnp.sum(grad_pre.astype(f32), axis=0, keepdims=True)
        if c == 0:
            branch_ref[...] = dot(hid, w_out)
            grad_ref[...] = dot(grad_pre, w_hidden)
        else:
            branch_ref[...] += dot(hid, w_out)
            grad_ref[...] += dot(grad_pre, w_hidden)
    out = ((mixed + branch_ref[...] + b_out_ref[...]) * mask).astype(bf16)
    for n in range(PAIR):
        store_row(plan, mixed_ref, out[n * plan.packed : (n + 1) * plan.packed], half, rows[n])
    grad_second = grad_ref[...]
    bump(gain_sum_ref, grad_second * xhat)
    bump(shift_sum_ref, grad_second)
    grad_mixed = grad_out + norm_back(grad_second * gain_two_ref[...], xhat, r)
    grad_mixed_ref[0] = grad_mixed
    bump(gain_one_sum_ref, grad_mixed * xhat_one)
    bump(shift_one_sum_ref, grad_mixed)
    for n in range(PAIR):
        keep_ref[rows[n]] = grad_mixed[n * plan.packed : (n + 1) * plan.packed].astype(bf16)

    for core in range(2):

        @pl.when((order == 0) & (pair == GROUP // PAIR - 1) & (d == core))
        def _():
            split_blocks(plan, send_ref, core * plan.blocks, [keep_ref[n] for n in range(GROUP)])

    @pl.when((order == 1) & (pair == GROUP // PAIR - 1))
    def _():
        split_blocks(plan, give_ref, 0, [keep_ref[n] for n in range(GROUP)])


def ffn_call(plan, slot, meta, frames, cot, recv, other, consts, kept):
    hidden = consts[4].shape[1]
    pairs = GROUP // PAIR
    tiles = HALVES * pairs
    height = PAIR * plan.packed
    token = pl.BlockSpec((height, plan.channels), lambda n, i: (slot * tiles + n * pairs + i, 0))
    wide = pl.BlockSpec((height, hidden), lambda n, i: (slot * tiles + n * pairs + i, 0))
    sums = [(1, plan.channels)] * 5 + [(1, hidden)]
    kept_shapes = [
        jax.ShapeDtypeStruct((plan.micro * tiles * height, n), bf16)
        for n in (plan.channels, plan.channels, hidden, hidden)
    ]
    own_shapes = [tile_shape(plan), packet_shape(plan, plan.places), packet_shape(plan, plan.blocks)]
    return pl.pallas_call(
        functools.partial(ffn_kernel, plan, hidden, len(kept)),
        grid=(HALVES, pairs),
        in_specs=[SCALARS, tile_spec(plan, slot), tile_spec(plan, slot), full(recv.shape), full(other.shape)]
        + [full(c.shape) for c in consts]
        + [pl.BlockSpec(memory_space=pl.ANY)] * len(kept),
        out_specs=[token, token, wide, wide]
        + [full(v.shape) for v in own_shapes]
        + [pl.BlockSpec((1, height, plan.channels), lambda n, i: (n * pairs + i, 0, 0))]
        + [full(v) for v in sums],
        out_shape=kept_shapes
        + own_shapes
        + [jax.ShapeDtypeStruct((tiles, height, plan.channels), f32)]
        + [jax.ShapeDtypeStruct(v, f32) for v in sums],
        scratch_shapes=[
            pltpu.VMEM((GROUP, plan.packed, plan.channels), bf16),
            pltpu.VMEM((GROUP, plan.packed, plan.channels), bf16),
            pltpu.VMEM((height, plan.channels), f32),
            pltpu.VMEM((height, plan.channels), f32),
        ],
        input_output_aliases={15 + n: n for n in range(len(kept))},
        compiler_params=params(60),
        cost_estimate=cost(45e9, 60e6),
    )(meta, frames, cot, recv, other, *consts, *kept)


def weight_kernel(near, second_ref, branch_grad_ref, hid_ref, pre_grad_ref, own_ref, other_ref):
    sums = [dot_tn(pre_grad_ref[...], second_ref[...]), dot_tn(hid_ref[...], branch_grad_ref[...])]
    for ref, mine in ((own_ref, pl.program_id(0) < near), (other_ref, pl.program_id(0) >= near)):

        @pl.when(mine)
        def _():
            for n in range(2):
                ref[0, n] = sums[n].astype(bf16)


def weight_call(kept, block):
    second, branch_grad, hid, pre_grad = kept
    tokens, channels = second.shape
    wide = pl.BlockSpec((tokens, block), lambda n: (0, n))
    near = hid.shape[1] // block // 2
    shape = (1, 2, block, channels)
    return pl.pallas_call(
        functools.partial(weight_kernel, near),
        grid=(2 * near,),
        in_specs=[full(second.shape), full(second.shape), wide, wide],
        out_specs=[
            pl.BlockSpec(shape, lambda n: (jnp.minimum(n, near - 1), 0, 0, 0)),
            pl.BlockSpec(shape, lambda n: (jnp.maximum(n - near, 0), 0, 0, 0)),
        ],
        out_shape=[jax.ShapeDtypeStruct((near,) + shape[1:], bf16)] * 2,
        compiler_params=params(48),
        cost_estimate=cost(22e9, 46e6),
    )(second, branch_grad, hid, pre_grad)


def last_kernel(plan, meta_ref, frames_ref, recv_ref, other_ref, grad_mixed_ref, gain_ref, out_ref):
    d = meta_ref[6]
    for n, ref, first in ((0, recv_ref, d * plan.blocks), (1, other_ref, 0)):
        half = d if n == 0 else 1 - d
        for i in range(GROUP):
            mask = row_mask(plan, meta_ref, half, i)
            xhat, r = statistics(load_row(plan, frames_ref, half, i).astype(f32) * mask)
            at = slice((i % PAIR) * plan.packed, (i % PAIR + 1) * plan.packed)
            grad_mixed = grad_mixed_ref[n * (GROUP // PAIR) + i // PAIR, at, :]
            grad_normed = join_blocks(plan, ref, first, i).astype(f32) + grad_mixed
            grad_inside = grad_mixed + norm_back(grad_normed * gain_ref[...], xhat, r)
            store_row(plan, out_ref, (grad_inside * mask).astype(bf16), half, i)


def last_call(plan, slot, meta, frames, recv, other, grad_mixed, gain):
    shape = tile_shape(plan)
    return pl.pallas_call(
        functools.partial(last_kernel, plan),
        grid=(1,),
        in_specs=[SCALARS, tile_spec(plan, slot)] + [full(v.shape) for v in (recv, other, grad_mixed, gain)],
        out_specs=full(shape.shape),
        out_shape=shape,
        compiler_params=params(40),
        cost_estimate=cost(8e9, 10e6),
    )(meta, frames, recv, other, grad_mixed, gain)


AXES = ("dp", "lon", "lat")


def exchange(values):
    return lax.all_to_all(values, ("lon", "lat"), 0, 0, tiled=True)


def swap(value, axis, bit):
    count = lax.axis_size(axis)
    return lax.ppermute(value, axis, [(n, n ^ bit) for n in range(count)])


def after(value, *others):
    return lax.optimization_barrier((value,) + others)[0]


def near(value, axis):
    return [value] + [swap(value, axis, d) for d in range(1, lax.axis_size(axis))]


def add(terms):
    return sum(v.astype(f32) for v in terms)


def near_to_place(value, axis, dim):
    count = lax.axis_size(axis)
    shape = value.shape
    bit = 1
    while bit < count:
        split = value.reshape(shape[:dim] + (count // (2 * bit), 2, bit) + shape[dim + 1 :])
        turned = jnp.flip(split, dim + 1)
        value = jnp.where((lax.axis_index(axis) & bit) == 0, split, turned).reshape(shape)
        bit *= 2
    return value


def sum_over(value, axis):
    bit = 1
    while bit < lax.axis_size(axis):
        value = value + swap(value, axis, bit)
        bit *= 2
    return value


def collect(value, axis, bits):
    for bit in bits:
        other = swap(value, axis, bit)
        low = (lax.axis_index(axis) & bit) == 0
        value = jnp.concatenate([jnp.where(low, value, other), jnp.where(low, other, value)], axis=0)
    return value


def body(
    frames,
    regions,
    cotangent,
    first_gain,
    first_shift,
    inner_weight,
    inner_bias,
    outer_weight,
    outer_bias,
    second_gain,
    second_shift,
    hidden_weight,
    hidden_bias,
    output_weight,
    output_bias,
):
    dp, lon, lat = (lax.axis_size(a) for a in AXES)
    dp_place, lon_place, lat_place = (lax.axis_index(a) for a in AXES)
    core = dp_place % 2
    micro, rows, cols, channels = frames.shape
    blocks = inner_weight.shape[0]
    plan = Plan(micro, rows, cols, channels, blocks, lat, lon)
    size = plan.size
    own_block = (lon_place * lat + lat_place) % blocks
    hidden_rows = hidden_weight.shape[0]
    hidden = hidden_rows * dp * lon * lat

    origin = jnp.stack([lat_place * rows, lon_place * cols, core]).astype(jnp.int32)
    metas = [jnp.concatenate([regions[s], origin]) for s in range(micro)]
    lon_table, lon_back_table = (jnp.asarray(t) for t in lon_tables(plan))
    pick = lambda t: lax.dynamic_index_in_dim(t, core, 0, keepdims=False)
    lon_back_table = pick(lon_back_table)
    tables = tuple(pick(jnp.asarray(t)) for t in lat_tables(plan))

    def row(v):
        return v.astype(f32).reshape(1, -1)

    def own(v):
        return lax.dynamic_index_in_dim(v, own_block, 0, keepdims=False)

    def padded(v):
        return jnp.pad(v, ((0, 0), (0, HALVES * plan.part - rows), (0, plan.padcol - cols), (0, 0)))

    def whole(parts):
        return jnp.stack(parts)[:, :rows, :cols]

    def join(send, give):
        return lax.dynamic_update_slice_in_dim(send, swap(give, "dp", 1), (1 - core) * blocks, 0)

    def other(received):
        return swap(lax.dynamic_slice_in_dim(received, (1 - core) * blocks, blocks, 0), "dp", 1)

    frame_tiles = padded(frames)
    cot_tiles = padded(cotangent)
    spectral_weights = (
        block_matrix(plan, own(inner_weight)),
        block_matrix(plan, own(outer_weight)),
        block_bias(plan, own(inner_bias)),
        block_bias(plan, own(outer_bias)),
    )
    slots = range(micro)

    bias_row = jnp.pad(hidden_bias.reshape(1, hidden_rows), ((0, 7), (0, channels - hidden_rows)))
    gathered = jnp.concatenate([hidden_weight, output_weight, bias_row], axis=0)
    metas[0] = after(metas[0], gathered)
    near_lat = jnp.stack(near(gathered, "lat"))
    gathered = lax.all_gather(near_lat, "lon", axis=0)
    gathered = gathered.reshape(lon * lat, -1, channels)
    done = (near_lat,)

    turn = []

    def queue(value):
        return after(value, *turn)

    def ran(output):
        turn[:] = [output]

    normed, sends = [], []
    for s in slots:
        send, give = first_call(plan, s, queue(metas[s]), frame_tiles, row(first_gain), row(first_shift))
        sends.append(join(send, give))
        ran(sends[-1])
        normed.append(exchange(after(sends[s], *done)))
        done = (normed[-1],)

    def start_waves(s, received):
        mine, give = lon_call(plan, metas[s], queue(received), lon_table)
        ran(mine)
        return mine, swap(give, "dp", 1)

    def waves_of(mine, other, middle, *args):
        mine, give, *rest = wave_call(plan, middle, queue(mine), other, tables, spectral_weights, *args)
        ran(mine)
        return (mine, swap(give, "dp", 1)), rest

    def field_of(mine, other, held=None):
        out = back_call(plan, queue(mine), other, lon_back_table, held)
        ran(out[0])
        return out

    def feed_forward_inputs(gathered):
        half = hidden // 2

        def gathered_rows(low):
            parts = near(gathered[:, low : low + hidden_rows].reshape(-1, channels), "dp")
            if dp == 2:
                return parts
            parts = jnp.concatenate(parts, axis=0)
            return [parts[:half], parts[half:]]

        b_hidden = jnp.stack(near(gathered[:, 2 * hidden_rows, :hidden_rows], "dp"))
        b_hidden = b_hidden.astype(f32).reshape(1, hidden)
        return (
            row(first_gain),
            row(first_shift),
            row(second_gain),
            row(second_shift),
            b_hidden,
            row(output_bias),
            *gathered_rows(0),
            *gathered_rows(hidden_rows),
        )

    filtered, kept_waves = [], []
    for s in slots:
        pair = start_waves(s, normed[s])
        if s + 1 == micro:
            gathered = after(gathered, pair[0])
            consts = feed_forward_inputs(gathered)
        pair, waves = waves_of(*pair, forward_middle, (), (bf16, bf16, bf16), False)
        kept_waves.append(waves)
        before = done + consts + (cot_tiles,) if s + 1 == micro else ()
        (send,) = field_of(after(pair[0], *before), pair[1])
        filtered.append(exchange(after(send, *done)))
        done = (filtered[-1],)

    kept = ()
    mixed, grad_mixed, grads, token_sums = [], [], [], []
    for s in slots:
        out = ffn_call(
            plan, s, queue(metas[s]), frame_tiles, cot_tiles, filtered[s], other(filtered[s]), consts, kept
        )
        kept = tuple(out[:4])
        mixed.append(out[4])
        joined = join(out[5], out[6])
        ran(joined)
        grads.append(exchange(after(joined, *done)))
        done = (grads[-1],)
        grad_mixed.append(out[7])
        token_sums.append(out[8:])
    token_sums = [sum(v) for v in zip(*token_sums)]
    hidden_bias_sum = token_sums.pop().reshape(dp, lon, lat, hidden_rows)
    hidden_bias_sum = near_to_place(near_to_place(hidden_bias_sum, "dp", 0), "lat", 2)

    block = 3 * LANES
    wave_sums, field_sums, sends = [], [], []
    parts = weight_call((queue(kept[0]),) + kept[1:], block)
    ran(parts[0])
    pair = start_waves(0, after(grads[0], *done))
    for s in slots:
        pair, waves = waves_of(*pair, backward_middle, kept_waves[s], (), True)
        wave_sums.append(waves)
        following = start_waves(s + 1, grads[s + 1]) if s + 1 < micro else None
        send, *sums = field_of(*pair, normed[s])
        field_sums.append(sums)
        sends.append(send)
        pair = following
    if dp == 2 and parts[0].shape[0] == lon:
        terms = [parts[0], after(swap(parts[1], "dp", 1), sends[0])]
    else:
        parts = jnp.concatenate(parts, axis=0).transpose(1, 0, 2, 3)
        parts = parts.reshape(2, dp, lon, lat * hidden_rows, channels).transpose(1, 2, 0, 3, 4)
        terms = [parts[0]] + [swap(parts[n], "dp", n) for n in range(1, dp)]
    own_part = add(terms).astype(bf16)
    lat_part = lax.psum_scatter(own_part.reshape(lon, -1, channels), "lon", scatter_dimension=0)
    lat_part = lat_part.reshape(2, lat, hidden_rows, channels)
    ffn_grads = add([lat_part[:, 0]] + [swap(lat_part[:, n], "lat", n) for n in range(1, lat)])
    product_sum, plain_sum = (sum(v) for v in zip(*field_sums))

    plain = jnp.sum(plain_sum.reshape(GROUP, size), axis=0)
    product = jnp.sum(product_sum.reshape(GROUP, size), axis=0)
    own_shift = own(first_shift.astype(f32).reshape(blocks, size))
    own_gain = own(first_gain.astype(f32).reshape(blocks, size))

    block_sums = sum(v[0] for v in wave_sums)
    bit = 2
    while bit < dp:
        block_sums = block_sums + swap(block_sums, "dp", bit)
        bit *= 2
    half_rows = block_sums.shape[0] // 2
    part_of = lambda n: lax.dynamic_slice_in_dim(block_sums, n * half_rows, half_rows, 0)
    block_sums = part_of(core) + swap(part_of(1 - core), "dp", 1)
    lon_blocks = blocks // lat
    bit = lon_blocks
    while bit < lon:
        block_sums = block_sums + swap(block_sums, "lon", bit)
        bit *= 2
    all_sums = block_sums[None]
    some_sums = all_sums
    all_sums = collect(all_sums, "lat", [1 << n for n in range(lat.bit_length() - 1)])
    all_sums = collect(all_sums, "lon", [1 << n for n in range(lon_blocks.bit_length() - 1)])
    all_sums = collect(all_sums[None], "dp", [1])
    all_sums = jnp.concatenate([all_sums[0], all_sums[1]], axis=1)
    all_sums = all_sums[:, :, :size]
    inner_grad = all_sums[:, : 2 * size].reshape(blocks, 2, size, size)
    outer_grad = all_sums[:, 2 * size : 4 * size].reshape(blocks, 2, size, size)
    base = 4 * size
    inner_bias_grad = all_sums[:, base : base + 2]
    outer_bias_grad = all_sums[:, base + 2 : base + 4]

    back, frame_grads = [], []
    for s in slots:
        last = s + 1 == micro
        back.append(exchange(after(sends[s], *done, *((some_sums,) if last else ()))))
        done = (back[-1],)
        if last:
            ran(ffn_grads)
        frame_grads.append(
            last_call(plan, s, queue(metas[s]), frame_tiles, back[s], other(back[s]), grad_mixed[s], row(first_gain))
        )
        ran(frame_grads[-1])

    def spread(value):
        return lax.dynamic_update_slice_in_dim(jnp.zeros((blocks, size), f32), value[None], own_block, 0)

    small = token_sums + [
        hidden_bias_sum,
        spread((product - own_shift * plain) / own_gain),
        spread(plain),
    ]
    small = jnp.concatenate([v.reshape(-1) for v in small]).reshape(-1, LANES)
    for axis in AXES:
        small = sum_over(small, axis)
    small = small.reshape(-1)
    second_gain_grad, second_shift_grad, output_bias_grad, gain_part, shift_part = (
        small[n * channels : (n + 1) * channels] for n in range(5)
    )
    order = lax.axis_index(AXES)
    hidden_bias_grad = lax.dynamic_slice_in_dim(small[5 * channels :], order * hidden_rows, hidden_rows, 0)
    base = 5 * channels + hidden
    first_gain_grad = gain_part + small[base : base + channels]
    first_shift_grad = shift_part + small[base + channels :]
    return (
        whole(mixed),
        whole(frame_grads),
        first_gain_grad,
        first_shift_grad,
        inner_grad,
        inner_bias_grad,
        outer_grad,
        outer_bias_grad,
        second_gain_grad,
        second_shift_grad,
        ffn_grads[0],
        hidden_bias_grad,
        ffn_grads[1],
        output_bias_grad,
    )


def solution(mesh):
    field = P("dp", "lat", "lon", None)
    rows = P(AXES, None)
    return jax.shard_map(
        body,
        mesh=mesh,
        in_specs=(field, P("dp", None), field) + (P(),) * 8 + (rows, P(AXES), rows, P()),
        out_specs=(field, field) + (P(),) * 8 + (rows, P(AXES), rows, P()),
        check_vma=False,
    )
```

```python
import functools
import math

import jax
import jax.numpy as jnp
import numpy as np
from jax import lax
from jax.experimental import pallas as pl
from jax.experimental.pallas import tpu as pltpu
from jax.sharding import PartitionSpec as P

H = 90
LANES = 128
GROUP = 4
HALVES = 2
MAX_KSTEP = 12
HINT = 0.05

epsilon = 1e-05
shrink_level = 0.01

f32 = jnp.float32
bf16 = jnp.bfloat16


class Plan:
    def __init__(self, micro, rows, cols, channels, blocks, lat, lon):
        self.micro, self.rows, self.cols, self.channels, self.blocks = micro, rows, cols, channels, blocks
        self.lat, self.lon = lat, lon
        self.places = lat * lon
        self.size = channels // blocks
        self.groups = -(-rows // (GROUP * HALVES))
        self.padcol = -(-cols // 16) * 16
        self.packed = self.groups * self.padcol
        self.part = self.groups * GROUP
        self.slots = lat * self.part
        self.pitch = odd_pitch(self.slots)
        self.height = rows * lat
        self.breadth = cols * lon
        self.waves = self.breadth // HALVES
        self.padwave = -(-self.waves // 16) * 16
        self.lanes = GROUP * self.size
        self.scale = float(H * self.breadth) ** (-0.5)
        self.kstep = max(k for k in range(2, MAX_KSTEP + 1, 2) if self.waves % k == 0)


def odd_pitch(rows):
    rows = -(-rows // 8) * 8
    return rows + 8 if rows % 16 == 0 else rows


def angle_tables(count, total):
    index = np.arange(total)
    turns = (index[:, None] * index[None, :]) % count
    angle = turns * (2.0 * math.pi / count)
    keep = ((index[:, None] < count) & (index[None, :] < count)).astype(np.float64)
    return np.cos(angle) * keep, np.sin(angle) * keep


def lon_tables(plan):
    cos, sin = angle_tables(plan.breadth, plan.breadth)
    width = plan.lon * plan.padcol
    out = np.zeros((2, plan.breadth, width), np.float32)
    for s in range(plan.lon):
        w = slice(s * plan.cols, (s + 1) * plan.cols)
        at = slice(s * plan.padcol, s * plan.padcol + plan.cols)
        out[0, :, at] = cos[:, w]
        out[1, :, at] = -sin[:, w]
    back = np.zeros((2, width, 2, 2, plan.padwave), np.float32)
    for d in range(2):
        for n in range(2):
            half = (d + n) % 2
            waves = slice(half * plan.waves, (half + 1) * plan.waves)
            for kind in range(2):
                back[d, :, n, kind, : plan.waves] = out[kind, waves].T
    return out.reshape(2 * plan.breadth, width).astype(jnp.bfloat16), back.reshape(2, width, -1).astype(jnp.bfloat16)


def lat_tables(plan):
    cos, sin = angle_tables(H, plan.height)
    n = HALVES * plan.slots
    forward, inverse = [], []
    for d in range(2):
        c = np.zeros((n, n))
        s = np.zeros((n, n))
        for order in range(2):
            half = (d + order) % 2
            for lat in range(plan.lat):
                for r in range(plan.part):
                    row = half * plan.part + r
                    if row < plan.rows:
                        at = order * plan.slots + lat * plan.part + r
                        c[: plan.height, at] = cos[:, lat * plan.rows + row]
                        s[: plan.height, at] = sin[:, lat * plan.rows + row]
        forward.append(np.block([[c, s], [-s, c]]))
        inverse.append(np.block([[c.T, -s.T], [s.T, c.T]]))
    return tuple(np.stack(t).astype(np.float32).astype(jnp.bfloat16) for t in (forward, inverse))


def dot(a, b):
    return lax.dot_general(a, b, (((1,), (0,)), ((), ())), preferred_element_type=f32)


def dot_nt(a, b):
    return lax.dot_general(a, b, (((1,), (1,)), ((), ())), preferred_element_type=f32)


def dot_tn(a, b):
    return lax.dot_general(a, b, (((0,), (0,)), ((), ())), preferred_element_type=f32)


def gelu_pair(x):
    phi = 0.5 + 0.5 * lax.erf(x * (0.5**0.5))
    density = jnp.exp(-0.5 * x * x) * (1.0 / math.sqrt(2.0 * math.pi))
    return x * phi, phi + x * density


def full(shape):
    return pl.BlockSpec(shape, lambda *_: (0,) * len(shape), pipeline_mode=pl.Buffered(1))


def params(mib):
    return pltpu.CompilerParams(vmem_limit_bytes=mib * 2**20)


def cost(flops, moved):
    return pl.CostEstimate(flops=int(flops * HINT), bytes_accessed=int(moved * HINT), transcendentals=0)


def bump(ref, value):
    ref[...] += jnp.sum(value, axis=0, keepdims=True)


def row_mask(plan, meta_ref, half, i):
    p = lax.broadcasted_iota(jnp.int32, (plan.packed, 1), 0)
    g = jnp.zeros_like(p)
    for t in range(1, plan.groups):
        g += (p >= plan.padcol * t).astype(jnp.int32)
    j = p - plan.padcol * g
    r = plan.part * half + GROUP * g + i
    h = meta_ref[4] + r
    w = meta_ref[5] + j
    d = w - meta_ref[2]
    d = jnp.where(d < 0, d + plan.breadth, d)
    inside = (
        (r < plan.rows)
        & (j < plan.cols)
        & (h >= meta_ref[0])
        & (h < meta_ref[0] + meta_ref[1])
        & (d < meta_ref[3])
    )
    return inside.astype(f32)


def load_row(plan, ref, half, i):
    base = plan.part * half + i
    return jnp.concatenate([ref[0, base + GROUP * g] for g in range(plan.groups)], axis=0)


def store_row(plan, ref, value, half, i):
    base = plan.part * half + i
    for g in range(plan.groups):
        ref[base + GROUP * g] = value[plan.padcol * g : plan.padcol * (g + 1)]


def statistics(x):
    centre = jnp.mean(x, axis=-1, keepdims=True)
    centred = x - centre
    spread = jnp.mean(centred * centred, axis=-1, keepdims=True)
    r = lax.rsqrt(spread + epsilon)
    return centred * r, r


def norm_back(g, xhat, r):
    return r * (g - jnp.mean(g, axis=-1, keepdims=True) - xhat * jnp.mean(g * xhat, axis=-1, keepdims=True))


def join_blocks(plan, ref, first, i):
    at = slice(i * plan.size, (i + 1) * plan.size)
    return jnp.concatenate([ref[first + b, :, at] for b in range(plan.blocks)], axis=1)


def split_blocks(plan, ref, first, values):
    for b in range(plan.blocks):
        at = slice(b * plan.size, (b + 1) * plan.size)
        ref[first + b] = jnp.concatenate([v[:, at] for v in values], axis=1)


SCALARS = pl.BlockSpec(memory_space=pltpu.SMEM)


def tile_spec(plan, slot):
    return pl.BlockSpec(
        (1, HALVES * plan.part, plan.padcol, plan.channels),
        lambda *_: (slot, 0, 0, 0),
        pipeline_mode=pl.Buffered(1),
    )


def tile_shape(plan):
    return jax.ShapeDtypeStruct((HALVES * plan.part, plan.padcol, plan.channels), bf16)


def packet_shape(plan, count):
    return jax.ShapeDtypeStruct((count, plan.packed, plan.lanes), bf16)


def first_kernel(plan, meta_ref, frames_ref, gain_ref, shift_ref, send_ref, give_ref):
    d = meta_ref[6]
    for n, ref, first in ((0, send_ref, d * plan.blocks), (1, give_ref, 0)):
        half = d if n == 0 else 1 - d
        values = []
        for i in range(GROUP):
            inside = load_row(plan, frames_ref, half, i).astype(f32) * row_mask(plan, meta_ref, half, i)
            xhat, _ = statistics(inside)
            values.append((xhat * gain_ref[...] + shift_ref[...]).astype(bf16))
        split_blocks(plan, ref, first, values)


def first_call(plan, slot, meta, frames, gain, shift):
    shapes = [packet_shape(plan, plan.places), packet_shape(plan, plan.blocks)]
    return pl.pallas_call(
        functools.partial(first_kernel, plan),
        grid=(1,),
        in_specs=[SCALARS, tile_spec(plan, slot), full(gain.shape), full(shift.shape)],
        out_specs=[full(v.shape) for v in shapes],
        out_shape=shapes,
        compiler_params=params(32),
        cost_estimate=cost(5e9, 8e6),
    )(meta, frames, gain, shift)


def lon_kernel(plan, meta_ref, recv_ref, table_ref, keep_ref, give_ref, wide_ref):
    g = pl.program_id(0)
    kinds, size, pad = 2 * plan.breadth, plan.size, plan.padcol
    at = pl.ds(pl.multiple_of(g * pad, 16), pad)
    gap = jnp.zeros((plan.lon * pad, LANES - size), bf16)
    for lat in range(plan.lat):
        rows = jnp.concatenate([recv_ref[lon * plan.lat + lat, at, :] for lon in range(plan.lon)], axis=0)
        for pair in range(GROUP // 2):
            pieces = []
            for i in (2 * pair, 2 * pair + 1):
                pieces += [rows[:, i * size : (i + 1) * size], gap]
            out = dot(table_ref[...], jnp.concatenate(pieces, axis=1))
            for n in range(2):
                slot = lat * plan.part + GROUP * g + 2 * pair + n
                wide_ref[pl.ds(slot, kinds, stride=plan.pitch), :] = out[:, n * LANES : (n + 1) * LANES]

    @pl.when(g == plan.groups - 1)
    def _():
        d = meta_ref[6]
        for ref, half in ((keep_ref, d), (give_ref, 1 - d)):
            for kind in range(2):
                base = kind * plan.breadth + half * plan.waves

                def move(k, _, ref=ref, kind=kind, base=base):
                    row = pl.multiple_of((base + k) * plan.pitch, 8)
                    to = pl.multiple_of(k * plan.slots, 16)
                    ref[kind, pl.ds(to, plan.slots), :] = wide_ref[pl.ds(row, plan.slots), :].astype(bf16)
                    return _

                lax.fori_loop(0, plan.waves, move, 0, unroll=10)


def lon_call(plan, meta, recv, table):
    shape = jax.ShapeDtypeStruct((2, plan.waves * plan.slots, LANES), bf16)
    return pl.pallas_call(
        functools.partial(lon_kernel, plan),
        grid=(plan.groups,),
        in_specs=[SCALARS, full(recv.shape), full(table.shape)],
        out_specs=[full(shape.shape)] * 2,
        out_shape=[shape] * 2,
        scratch_shapes=[pltpu.VMEM((2 * plan.breadth * plan.pitch, LANES), f32)],
        compiler_params=params(40),
        cost_estimate=cost(4e9, 8e6),
    )(meta, recv, table)


def wave_kernel(plan, middle, counts, *refs):
    refs = list(refs)

    def take(n):
        got = tuple(refs[:n])
        del refs[:n]
        return got

    mine_ref, other_ref, lat_ref, lat_back_ref = take(4)
    weights = take(4)
    ins = take(counts[0])
    back_refs = take(2)
    outs = take(counts[1])
    totals = take(counts[2])
    tall_refs = refs[:2]
    sums_ref = totals[0] if totals else None
    totals = tuple(refs[2:])
    step = pl.program_id(0)
    slots, pitch = plan.slots, odd_pitch(2 * plan.padwave)
    both = HALVES * slots

    @pl.when(step == 0)
    def _():
        for ref in totals + tuple(tall_refs):
            ref[...] = jnp.zeros_like(ref)

    spectra = []
    for pair in range(plan.kstep // 2):
        columns = []
        for n in range(2):
            at = slice((2 * pair + n) * slots, (2 * pair + n + 1) * slots)
            columns.append(
                jnp.concatenate([ref[kind, at, :] for kind in range(2) for ref in (mine_ref, other_ref)], axis=0)
            )
        out = dot(lat_ref[...], jnp.concatenate(columns, axis=1)) * plan.scale
        for n in range(2):
            at = slice(n * LANES, (n + 1) * LANES)
            spectra.append(jnp.concatenate([out[:both, at], out[both:, at]], axis=1))
    result = middle(jnp.concatenate(spectra, axis=0), weights, ins, outs, totals)
    for pair in range(plan.kstep // 2):
        columns = []
        for n in range(2):
            at = slice((2 * pair + n) * both, (2 * pair + n + 1) * both)
            columns.append(jnp.concatenate([result[at, :LANES], result[at, LANES:]], axis=0))
        out = dot(lat_back_ref[...], jnp.concatenate(columns, axis=1)) * plan.scale
        for n in range(2):
            k = step * plan.kstep + 2 * pair + n
            at = slice(n * LANES, (n + 1) * LANES)
            for kind in range(2):
                for order in range(2):
                    low = kind * both + order * slots
                    tall_refs[order][pl.ds(kind * plan.padwave + k, slots, stride=pitch), :] = out[
                        low : low + slots, at
                    ]

    @pl.when(step == pl.num_programs(0) - 1)
    def _():
        for ref, tall_ref in zip(back_refs, tall_refs):

            def move(h, _, ref=ref, tall_ref=tall_ref):
                row = pl.multiple_of(h * pitch, 8)
                to = pl.multiple_of(h * 2 * plan.padwave, 16)
                ref[pl.ds(to, 2 * plan.padwave), :] = tall_ref[pl.ds(row, 2 * plan.padwave), :].astype(bf16)
                return _

            lax.fori_loop(0, slots, move, 0, unroll=4)

        if totals:
            size = plan.size
            low, high = slice(0, size), slice(LANES, LANES + size)
            for n, total in enumerate(totals[:2]):
                base = 2 * size * n
                sums_ref[base : base + size] = total[low, :LANES] + total[high, LANES:]
                sums_ref[base + size : base + 2 * size] = total[low, LANES:] - total[high, :LANES]
            rows = [total[:, at] for total in totals[2:] for at in (slice(0, LANES), slice(LANES, None))]
            rows.append(jnp.zeros((sums_ref.shape[0] - 4 * size - 4, LANES), f32))
            sums_ref[4 * size :] = jnp.concatenate(rows, axis=0)


def sum_rows(plan):
    return -(-(4 * plan.size + 4) // 16) * 16


def wave_call(plan, middle, mine, other, tables, weights, streams_in, out_types, sums):
    consts = tables + weights
    part = pl.BlockSpec((2, plan.kstep * plan.slots, LANES), lambda s: (0, s, 0))
    stream = pl.BlockSpec((plan.kstep * HALVES * plan.slots, 2 * LANES), lambda s: (s, 0))
    sum_shapes = [(sum_rows(plan), LANES)] if sums else []
    total_shapes = [(2 * LANES, 2 * LANES)] * 2 + [(1, 2 * LANES)] * 2 if sums else []
    back = jax.ShapeDtypeStruct((plan.slots * 2 * plan.padwave, LANES), bf16)
    rows = plan.waves * HALVES * plan.slots
    return pl.pallas_call(
        functools.partial(wave_kernel, plan, middle, (len(streams_in), len(out_types), len(sum_shapes))),
        grid=(plan.waves // plan.kstep,),
        in_specs=[part] * 2 + [full(c.shape) for c in consts] + [stream] * len(streams_in),
        out_specs=[full(back.shape)] * 2 + [stream] * len(out_types) + [full(s) for s in sum_shapes],
        out_shape=[back] * 2
        + [jax.ShapeDtypeStruct((rows, 2 * LANES), t) for t in out_types]
        + [jax.ShapeDtypeStruct(s, f32) for s in sum_shapes],
        scratch_shapes=[pltpu.VMEM((plan.slots * odd_pitch(2 * plan.padwave), LANES), f32)] * 2
        + [pltpu.VMEM(v, f32) for v in total_shapes],
        compiler_params=params(48),
        cost_estimate=cost(20e9, 24e6),
    )(mine, other, *consts, *streams_in)


def back_kernel(plan, summed, mine_ref, other_ref, table_ref, *refs):
    g = pl.program_id(0)
    held_ref = refs[0] if summed else None
    send_ref = refs[1 if summed else 0]
    totals = refs[2:] if summed else ()
    kinds, size, pad = 2 * plan.padwave, plan.size, plan.padcol
    rows = pl.ds(pl.multiple_of(g * pad, 16), pad)

    if summed:

        @pl.when(g == 0)
        def _():
            for total in totals:
                total[...] = jnp.zeros_like(total)

    for lat in range(plan.lat):
        pieces = []
        for pair in range(GROUP // 2):
            columns = []
            for i in (2 * pair, 2 * pair + 1):
                at = pl.ds(pl.multiple_of((lat * plan.part + GROUP * g + i) * kinds, 16), kinds)
                columns.append(jnp.concatenate([mine_ref[at, :], other_ref[at, :]], axis=0))
            out = dot(table_ref[...], jnp.concatenate(columns, axis=1)).astype(bf16)
            pieces += [out[:, :size], out[:, LANES : LANES + size]]
        out = jnp.concatenate(pieces, axis=1)
        for lon in range(plan.lon):
            source = lon * plan.lat + lat
            value = out[lon * pad : (lon + 1) * pad]
            send_ref[source, rows, :] = value
            if summed:
                value = value.astype(f32)
                bump(totals[0], value * held_ref[source, rows, :].astype(f32))
                bump(totals[1], value)


def back_call(plan, mine, other, table, held=None):
    consts = (mine, other, table) + (() if held is None else (held,))
    shapes = [packet_shape(plan, plan.places)]
    if held is not None:
        shapes += [jax.ShapeDtypeStruct((1, plan.lanes), f32)] * 2
    return pl.pallas_call(
        functools.partial(back_kernel, plan, held is not None),
        grid=(plan.groups,),
        in_specs=[full(c.shape) for c in consts],
        out_specs=[full(v.shape) for v in shapes],
        out_shape=shapes,
        compiler_params=params(32),
        cost_estimate=cost(4e9, 8e6),
    )(*consts)


def forward_middle(freq, weights, ins, outs, totals):
    w_in_ref, w_out_ref, b_in_ref, b_out_ref = weights
    freq_ref, hid_ref, slope_ref = outs
    freq = freq.astype(bf16)
    freq_ref[...] = freq
    hid, slope = gelu_pair(dot(freq, w_in_ref[...]) + b_in_ref[...])
    hid = hid.astype(bf16)
    hid_ref[...] = hid
    slope_ref[...] = slope.astype(slope_ref.dtype)
    out = dot(hid, w_out_ref[...]) + b_out_ref[...]
    return (out - shrink_level * out * lax.rsqrt(out * out + shrink_level * shrink_level)).astype(bf16)


def backward_middle(grad_spec, weights, ins, outs, totals):
    w_in_ref, w_out_ref, b_in_ref, b_out_ref = weights
    freq_ref, hid_ref, slope_ref = ins
    in_sum_ref, out_sum_ref, in_bias_ref, out_bias_ref = totals
    hid = hid_ref[...]
    out = dot(hid, w_out_ref[...]) + b_out_ref[...]
    r = lax.rsqrt(out * out + shrink_level * shrink_level)
    grad_out = (grad_spec * (1.0 - shrink_level**3 * (r * r * r))).astype(bf16)
    out_sum_ref[...] += dot_tn(hid, grad_out)
    bump(out_bias_ref, grad_out.astype(f32))
    grad_pre = (dot_nt(grad_out, w_out_ref[...]) * slope_ref[...].astype(f32)).astype(bf16)
    in_sum_ref[...] += dot_tn(freq_ref[...], grad_pre)
    bump(in_bias_ref, grad_pre.astype(f32))
    return dot_nt(grad_pre, w_in_ref[...]).astype(bf16)


def block_matrix(plan, weight):
    pad = ((0, LANES - plan.size), (0, LANES - plan.size))
    real = jnp.pad(weight[0], pad)
    imag = jnp.pad(weight[1], pad)
    return jnp.concatenate(
        [jnp.concatenate([real, imag], axis=1), jnp.concatenate([-imag, real], axis=1)], axis=0
    )


def block_bias(plan, bias):
    return jnp.pad(bias.astype(f32), ((0, 0), (0, LANES - plan.size))).reshape(1, 2 * LANES)


FCHUNK = 512
PAIR = 2


def ffn_kernel(plan, hidden, kept, *refs):
    (
        meta_ref,
        frames_ref,
        cot_ref,
        recv_ref,
        other_ref,
        gain_one_ref,
        shift_one_ref,
        gain_two_ref,
        shift_two_ref,
        b_hidden_ref,
        b_out_ref,
        *weight_refs,
    ) = refs[:15]
    (
        second_ref,
        branch_grad_ref,
        hid_ref,
        pre_grad_ref,
        mixed_ref,
        send_ref,
        give_ref,
        grad_mixed_ref,
        gain_sum_ref,
        shift_sum_ref,
        out_bias_sum_ref,
        gain_one_sum_ref,
        shift_one_sum_ref,
        hidden_bias_sum_ref,
        filt_ref,
        keep_ref,
        branch_ref,
        grad_ref,
    ) = refs[15 + kept :]
    order, pair = pl.program_id(0), pl.program_id(1)
    d = meta_ref[6]
    half = jnp.where(order == 0, d, 1 - d)
    rows = [PAIR * pair + n for n in range(PAIR)]

    @pl.when((order == 0) & (pair == 0))
    def _():
        for ref in (
            gain_sum_ref,
            shift_sum_ref,
            out_bias_sum_ref,
            gain_one_sum_ref,
            shift_one_sum_ref,
            hidden_bias_sum_ref,
        ):
            ref[...] = jnp.zeros_like(ref)

    @pl.when((order == 0) & (pair == 0))
    def _():
        for n in range(GROUP):
            filt_ref[n] = join_blocks(plan, recv_ref, d * plan.blocks, n)

    @pl.when((order == 1) & (pair == 0))
    def _():
        for n in range(GROUP):
            filt_ref[n] = join_blocks(plan, other_ref, 0, n)

    def tile(load):
        return jnp.concatenate([load(i) for i in rows], axis=0)

    mask = tile(lambda i: row_mask(plan, meta_ref, half, i))
    inside = tile(lambda i: load_row(plan, frames_ref, half, i)).astype(f32) * mask
    xhat_one, _ = statistics(inside)
    normed = xhat_one * gain_one_ref[...] + shift_one_ref[...]
    mixed = tile(lambda i: filt_ref[i]).astype(f32) + normed + inside
    xhat, r = statistics(mixed)
    second = (xhat * gain_two_ref[...] + shift_two_ref[...]).astype(bf16)
    second_ref[...] = second
    grad_out = tile(lambda i: load_row(plan, cot_ref, half, i)).astype(f32) * mask
    grad_branch = grad_out.astype(bf16)
    branch_grad_ref[...] = grad_branch
    bump(out_bias_sum_ref, grad_branch.astype(f32))
    for c in range(hidden // FCHUNK):
        at = slice(c * FCHUNK, (c + 1) * FCHUNK)
        which, low = divmod(c * FCHUNK, hidden // 2)
        w_hidden = weight_refs[which][low : low + FCHUNK, :]
        w_out = weight_refs[2 + which][low : low + FCHUNK, :]
        hid, slope = gelu_pair(dot_nt(second, w_hidden) + b_hidden_ref[:, at])
        hid = hid.astype(bf16)
        hid_ref[:, at] = hid
        grad_pre = (dot_nt(grad_branch, w_out) * slope).astype(bf16)
        pre_grad_ref[:, at] = grad_pre
        hidden_bias_sum_ref[:, at] += jnp.sum(grad_pre.astype(f32), axis=0, keepdims=True)
        if c == 0:
            branch_ref[...] = dot(hid, w_out)
            grad_ref[...] = dot(grad_pre, w_hidden)
        else:
            branch_ref[...] += dot(hid, w_out)
            grad_ref[...] += dot(grad_pre, w_hidden)
    out = ((mixed + branch_ref[...] + b_out_ref[...]) * mask).astype(bf16)
    for n in range(PAIR):
        store_row(plan, mixed_ref, out[n * plan.packed : (n + 1) * plan.packed], half, rows[n])
    grad_second = grad_ref[...]
    bump(gain_sum_ref, grad_second * xhat)
    bump(shift_sum_ref, grad_second)
    grad_mixed = grad_out + norm_back(grad_second * gain_two_ref[...], xhat, r)
    grad_mixed_ref[0] = grad_mixed
    bump(gain_one_sum_ref, grad_mixed * xhat_one)
    bump(shift_one_sum_ref, grad_mixed)
    for n in range(PAIR):
        keep_ref[rows[n]] = grad_mixed[n * plan.packed : (n + 1) * plan.packed].astype(bf16)

    for core in range(2):

        @pl.when((order == 0) & (pair == GROUP // PAIR - 1) & (d == core))
        def _():
            split_blocks(plan, send_ref, core * plan.blocks, [keep_ref[n] for n in range(GROUP)])

    @pl.when((order == 1) & (pair == GROUP // PAIR - 1))
    def _():
        split_blocks(plan, give_ref, 0, [keep_ref[n] for n in range(GROUP)])


def ffn_call(plan, slot, meta, frames, cot, recv, other, consts, kept):
    hidden = consts[4].shape[1]
    pairs = GROUP // PAIR
    tiles = HALVES * pairs
    height = PAIR * plan.packed
    token = pl.BlockSpec((height, plan.channels), lambda n, i: (slot * tiles + n * pairs + i, 0))
    wide = pl.BlockSpec((height, hidden), lambda n, i: (slot * tiles + n * pairs + i, 0))
    sums = [(1, plan.channels)] * 5 + [(1, hidden)]
    kept_shapes = [
        jax.ShapeDtypeStruct((plan.micro * tiles * height, n), bf16)
        for n in (plan.channels, plan.channels, hidden, hidden)
    ]
    own_shapes = [tile_shape(plan), packet_shape(plan, plan.places), packet_shape(plan, plan.blocks)]
    return pl.pallas_call(
        functools.partial(ffn_kernel, plan, hidden, len(kept)),
        grid=(HALVES, pairs),
        in_specs=[SCALARS, tile_spec(plan, slot), tile_spec(plan, slot), full(recv.shape), full(other.shape)]
        + [full(c.shape) for c in consts]
        + [pl.BlockSpec(memory_space=pl.ANY)] * len(kept),
        out_specs=[token, token, wide, wide]
        + [full(v.shape) for v in own_shapes]
        + [pl.BlockSpec((1, height, plan.channels), lambda n, i: (n * pairs + i, 0, 0))]
        + [full(v) for v in sums],
        out_shape=kept_shapes
        + own_shapes
        + [jax.ShapeDtypeStruct((tiles, height, plan.channels), f32)]
        + [jax.ShapeDtypeStruct(v, f32) for v in sums],
        scratch_shapes=[
            pltpu.VMEM((GROUP, plan.packed, plan.channels), bf16),
            pltpu.VMEM((GROUP, plan.packed, plan.channels), bf16),
            pltpu.VMEM((height, plan.channels), f32),
            pltpu.VMEM((height, plan.channels), f32),
        ],
        input_output_aliases={15 + n: n for n in range(len(kept))},
        compiler_params=params(60),
        cost_estimate=cost(45e9, 60e6),
    )(meta, frames, cot, recv, other, *consts, *kept)


def weight_kernel(near, second_ref, branch_grad_ref, hid_ref, pre_grad_ref, own_ref, *other_refs):
    step = pl.program_id(0)
    sums = [dot_tn(pre_grad_ref[...], second_ref[...]), dot_tn(hid_ref[...], branch_grad_ref[...])]

    @pl.when(step < near)
    def _():
        for n in range(2):
            own_ref[0, n] = sums[n].astype(bf16)

    for m, ref in enumerate(other_refs):

        @pl.when(step == near + m)
        def _():
            for n in range(2):
                ref[n] = sums[n].astype(bf16)


def weight_call(kept, block):
    second, branch_grad, hid, pre_grad = kept
    tokens, channels = second.shape
    wide = pl.BlockSpec((tokens, block), lambda n: (0, n))
    near = hid.shape[1] // block // 2
    shape = (2, block, channels)
    return pl.pallas_call(
        functools.partial(weight_kernel, near),
        grid=(2 * near,),
        in_specs=[full(second.shape), full(second.shape), wide, wide],
        out_specs=[pl.BlockSpec((1,) + shape, lambda n: (jnp.minimum(n, near - 1), 0, 0, 0))]
        + [full(shape)] * near,
        out_shape=[jax.ShapeDtypeStruct((near,) + shape, bf16)] + [jax.ShapeDtypeStruct(shape, bf16)] * near,
        compiler_params=params(48),
        cost_estimate=cost(22e9, 46e6),
    )(second, branch_grad, hid, pre_grad)


def last_kernel(plan, meta_ref, frames_ref, recv_ref, other_ref, grad_mixed_ref, gain_ref, out_ref):
    d = meta_ref[6]
    for n, ref, first in ((0, recv_ref, d * plan.blocks), (1, other_ref, 0)):
        half = d if n == 0 else 1 - d
        for i in range(GROUP):
            mask = row_mask(plan, meta_ref, half, i)
            xhat, r = statistics(load_row(plan, frames_ref, half, i).astype(f32) * mask)
            at = slice((i % PAIR) * plan.packed, (i % PAIR + 1) * plan.packed)
            grad_mixed = grad_mixed_ref[n * (GROUP // PAIR) + i // PAIR, at, :]
            grad_normed = join_blocks(plan, ref, first, i).astype(f32) + grad_mixed
            grad_inside = grad_mixed + norm_back(grad_normed * gain_ref[...], xhat, r)
            store_row(plan, out_ref, (grad_inside * mask).astype(bf16), half, i)


def last_call(plan, slot, meta, frames, recv, other, grad_mixed, gain):
    shape = tile_shape(plan)
    return pl.pallas_call(
        functools.partial(last_kernel, plan),
        grid=(1,),
        in_specs=[SCALARS, tile_spec(plan, slot)] + [full(v.shape) for v in (recv, other, grad_mixed, gain)],
        out_specs=full(shape.shape),
        out_shape=shape,
        compiler_params=params(40),
        cost_estimate=cost(8e9, 10e6),
    )(meta, frames, recv, other, grad_mixed, gain)


AXES = ("dp", "lon", "lat")


def exchange(values):
    return lax.all_to_all(values, ("lon", "lat"), 0, 0, tiled=True)


def swap(value, axis, bit):
    count = lax.axis_size(axis)
    return lax.ppermute(value, axis, [(n, n ^ bit) for n in range(count)])


def after(value, *others):
    return lax.optimization_barrier((value,) + others)[0]


def near(value, axis):
    return [value] + [swap(value, axis, d) for d in range(1, lax.axis_size(axis))]


def add(terms):
    return sum(v.astype(f32) for v in terms)


def near_to_place(value, axis, dim):
    count = lax.axis_size(axis)
    shape = value.shape
    bit = 1
    while bit < count:
        split = value.reshape(shape[:dim] + (count // (2 * bit), 2, bit) + shape[dim + 1 :])
        turned = jnp.flip(split, dim + 1)
        value = jnp.where((lax.axis_index(axis) & bit) == 0, split, turned).reshape(shape)
        bit *= 2
    return value


def sum_over(value, axis):
    bit = 1
    while bit < lax.axis_size(axis):
        value = value + swap(value, axis, bit)
        bit *= 2
    return value


def collect(value, axis, bits):
    for bit in bits:
        other = swap(value, axis, bit)
        low = (lax.axis_index(axis) & bit) == 0
        value = jnp.concatenate([jnp.where(low, value, other), jnp.where(low, other, value)], axis=0)
    return value


def body(
    frames,
    regions,
    cotangent,
    first_gain,
    first_shift,
    inner_weight,
    inner_bias,
    outer_weight,
    outer_bias,
    second_gain,
    second_shift,
    hidden_weight,
    hidden_bias,
    output_weight,
    output_bias,
):
    dp, lon, lat = (lax.axis_size(a) for a in AXES)
    dp_place, lon_place, lat_place = (lax.axis_index(a) for a in AXES)
    core = dp_place % 2
    micro, rows, cols, channels = frames.shape
    blocks = inner_weight.shape[0]
    plan = Plan(micro, rows, cols, channels, blocks, lat, lon)
    size = plan.size
    own_block = (lon_place * lat + lat_place) % blocks
    hidden_rows = hidden_weight.shape[0]
    hidden = hidden_rows * dp * lon * lat

    origin = jnp.stack([lat_place * rows, lon_place * cols, core]).astype(jnp.int32)
    metas = [jnp.concatenate([regions[s], origin]) for s in range(micro)]
    lon_table, lon_back_table = (jnp.asarray(t) for t in lon_tables(plan))
    pick = lambda t: lax.dynamic_index_in_dim(t, core, 0, keepdims=False)
    lon_back_table = pick(lon_back_table)
    tables = tuple(pick(jnp.asarray(t)) for t in lat_tables(plan))

    def row(v):
        return v.astype(f32).reshape(1, -1)

    def own(v):
        return lax.dynamic_index_in_dim(v, own_block, 0, keepdims=False)

    def padded(v):
        return jnp.pad(v, ((0, 0), (0, HALVES * plan.part - rows), (0, plan.padcol - cols), (0, 0)))

    def whole(parts):
        return jnp.stack(parts)[:, :rows, :cols]

    def join(send, give):
        return lax.dynamic_update_slice_in_dim(send, swap(give, "dp", 1), (1 - core) * blocks, 0)

    def other(received):
        return swap(lax.dynamic_slice_in_dim(received, (1 - core) * blocks, blocks, 0), "dp", 1)

    frame_tiles = padded(frames)
    cot_tiles = padded(cotangent)
    spectral_weights = (
        block_matrix(plan, own(inner_weight)),
        block_matrix(plan, own(outer_weight)),
        block_bias(plan, own(inner_bias)),
        block_bias(plan, own(outer_bias)),
    )
    slots = range(micro)

    bias_row = jnp.pad(hidden_bias.reshape(1, hidden_rows), ((0, 7), (0, channels - hidden_rows)))
    gathered = jnp.concatenate([hidden_weight, output_weight, bias_row], axis=0)
    metas[0] = after(metas[0], gathered)
    near_lat = jnp.stack(near(gathered, "lat"))
    gathered = lax.all_gather(near_lat, "lon", axis=0)
    gathered = gathered.reshape(lon * lat, -1, channels)
    done = (near_lat,)

    turn = []

    def queue(value):
        return after(value, *turn)

    def ran(output):
        turn[:] = [output]

    normed, sends = [], []
    for s in slots:
        send, give = first_call(plan, s, queue(metas[s]), frame_tiles, row(first_gain), row(first_shift))
        sends.append(join(send, give))
        ran(sends[-1])
        normed.append(exchange(after(sends[s], *done)))
        done = (normed[-1],)

    def start_waves(s, received):
        mine, give = lon_call(plan, metas[s], queue(received), lon_table)
        ran(mine)
        return mine, swap(give, "dp", 1)

    def waves_of(mine, other, middle, *args):
        mine, give, *rest = wave_call(plan, middle, queue(mine), other, tables, spectral_weights, *args)
        ran(mine)
        return (mine, swap(give, "dp", 1)), rest

    def field_of(mine, other, held=None):
        out = back_call(plan, queue(mine), other, lon_back_table, held)
        ran(out[0])
        return out

    def feed_forward_inputs(gathered):
        half = hidden // 2

        def gathered_rows(low):
            parts = near(gathered[:, low : low + hidden_rows].reshape(-1, channels), "dp")
            if dp == 2:
                return parts
            parts = jnp.concatenate(parts, axis=0)
            return [parts[:half], parts[half:]]

        b_hidden = jnp.stack(near(gathered[:, 2 * hidden_rows, :hidden_rows], "dp"))
        b_hidden = b_hidden.astype(f32).reshape(1, hidden)
        return (
            row(first_gain),
            row(first_shift),
            row(second_gain),
            row(second_shift),
            b_hidden,
            row(output_bias),
            *gathered_rows(0),
            *gathered_rows(hidden_rows),
        )

    filtered, kept_waves = [], []
    for s in slots:
        pair = start_waves(s, normed[s])
        if s + 1 == micro:
            gathered = after(gathered, pair[0])
            consts = feed_forward_inputs(gathered)
        pair, waves = waves_of(*pair, forward_middle, (), (bf16, bf16, bf16), False)
        kept_waves.append(waves)
        before = done + consts + (cot_tiles,) if s + 1 == micro else ()
        (send,) = field_of(after(pair[0], *before), pair[1])
        filtered.append(exchange(after(send, *done)))
        done = (filtered[-1],)

    kept = ()
    mixed, grad_mixed, grads, token_sums = [], [], [], []
    for s in slots:
        out = ffn_call(
            plan, s, queue(metas[s]), frame_tiles, cot_tiles, filtered[s], other(filtered[s]), consts, kept
        )
        kept = tuple(out[:4])
        mixed.append(out[4])
        joined = join(out[5], out[6])
        ran(joined)
        grads.append(exchange(after(joined, *done)))
        done = (grads[-1],)
        grad_mixed.append(out[7])
        token_sums.append(out[8:])
    token_sums = [sum(v) for v in zip(*token_sums)]
    hidden_bias_sum = token_sums.pop().reshape(dp, lon, lat, hidden_rows)
    hidden_bias_sum = near_to_place(near_to_place(hidden_bias_sum, "dp", 0), "lat", 2)

    block = 3 * LANES
    wave_sums, field_sums, sends = [], [], []
    parts = weight_call((queue(kept[0]),) + kept[1:], block)
    ran(parts[0])
    pair = start_waves(0, after(grads[0], *done))
    if dp == 2 and parts[0].shape[0] == lon:
        terms = [parts[0], jnp.stack([swap(v, "dp", 1) for v in parts[1:]])]
    else:
        parts = jnp.concatenate([parts[0], jnp.stack(parts[1:])], axis=0).transpose(1, 0, 2, 3)
        parts = parts.reshape(2, dp, lon, lat * hidden_rows, channels).transpose(1, 2, 0, 3, 4)
        terms = [parts[0]] + [swap(parts[n], "dp", n) for n in range(1, dp)]
    own_part = add(terms).astype(bf16)
    own_part, ahead = lax.optimization_barrier((own_part, pair[0]))
    pair = (ahead, pair[1])
    for s in slots:
        pair, waves = waves_of(*pair, backward_middle, kept_waves[s], (), True)
        wave_sums.append(waves)
        following = start_waves(s + 1, grads[s + 1]) if s + 1 < micro else None
        send, *sums = field_of(*pair, normed[s])
        field_sums.append(sums)
        sends.append(send)
        pair = following
    lat_part = lax.psum_scatter(own_part.reshape(lon, -1, channels), "lon", scatter_dimension=0)
    lat_part = lat_part.reshape(2, lat, hidden_rows, channels)
    ffn_grads = add([lat_part[:, 0]] + [swap(lat_part[:, n], "lat", n) for n in range(1, lat)])
    product_sum, plain_sum = (sum(v) for v in zip(*field_sums))

    plain = jnp.sum(plain_sum.reshape(GROUP, size), axis=0)
    product = jnp.sum(product_sum.reshape(GROUP, size), axis=0)
    own_shift = own(first_shift.astype(f32).reshape(blocks, size))
    own_gain = own(first_gain.astype(f32).reshape(blocks, size))

    block_sums = sum(v[0] for v in wave_sums)
    bit = 2
    while bit < dp:
        block_sums = block_sums + swap(block_sums, "dp", bit)
        bit *= 2
    half_rows = block_sums.shape[0] // 2
    part_of = lambda n: lax.dynamic_slice_in_dim(block_sums, n * half_rows, half_rows, 0)
    block_sums = part_of(core) + swap(part_of(1 - core), "dp", 1)
    lon_blocks = blocks // lat
    bit = lon_blocks
    while bit < lon:
        block_sums = block_sums + swap(block_sums, "lon", bit)
        bit *= 2
    all_sums = block_sums[None]
    some_sums = all_sums
    all_sums = collect(all_sums, "lat", [1 << n for n in range(lat.bit_length() - 1)])
    all_sums = collect(all_sums, "lon", [1 << n for n in range(lon_blocks.bit_length() - 1)])
    all_sums = collect(after(all_sums[None], ffn_grads), "dp", [1])
    all_sums = jnp.concatenate([all_sums[0], all_sums[1]], axis=1)
    all_sums = all_sums[:, :, :size]
    inner_grad = all_sums[:, : 2 * size].reshape(blocks, 2, size, size)
    outer_grad = all_sums[:, 2 * size : 4 * size].reshape(blocks, 2, size, size)
    base = 4 * size
    inner_bias_grad = all_sums[:, base : base + 2]
    outer_bias_grad = all_sums[:, base + 2 : base + 4]

    back, frame_grads = [], []
    for s in slots:
        last = s + 1 == micro
        back.append(exchange(after(sends[s], *done, *((some_sums,) if last else ()))))
        done = (back[-1],)
        frame_grads.append(
            last_call(plan, s, queue(metas[s]), frame_tiles, back[s], other(back[s]), grad_mixed[s], row(first_gain))
        )
        ran(frame_grads[-1])

    def spread(value):
        return lax.dynamic_update_slice_in_dim(jnp.zeros((blocks, size), f32), value[None], own_block, 0)

    small = token_sums + [
        hidden_bias_sum,
        spread((product - own_shift * plain) / own_gain),
        spread(plain),
    ]
    small = jnp.concatenate([v.reshape(-1) for v in small]).reshape(-1, LANES)
    for axis in AXES:
        small = sum_over(small, axis)
    small = small.reshape(-1)
    second_gain_grad, second_shift_grad, output_bias_grad, gain_part, shift_part = (
        small[n * channels : (n + 1) * channels] for n in range(5)
    )
    order = lax.axis_index(AXES)
    hidden_bias_grad = lax.dynamic_slice_in_dim(small[5 * channels :], order * hidden_rows, hidden_rows, 0)
    base = 5 * channels + hidden
    first_gain_grad = gain_part + small[base : base + channels]
    first_shift_grad = shift_part + small[base + channels :]
    return (
        whole(mixed),
        whole(frame_grads),
        first_gain_grad,
        first_shift_grad,
        inner_grad,
        inner_bias_grad,
        outer_grad,
        outer_bias_grad,
        second_gain_grad,
        second_shift_grad,
        ffn_grads[0],
        hidden_bias_grad,
        ffn_grads[1],
        output_bias_grad,
    )


def solution(mesh):
    field = P("dp", "lat", "lon", None)
    rows = P(AXES, None)
    return jax.shard_map(
        body,
        mesh=mesh,
        in_specs=(field, P("dp", None), field) + (P(),) * 8 + (rows, P(AXES), rows, P()),
        out_specs=(field, field) + (P(),) * 8 + (rows, P(AXES), rows, P()),
        check_vma=False,
    )
```
